32 devices in a mesh: seq: 8 (over y, x, core), head: 4 (over z).
Axes of the slice: x: 2, y: 2, z: 4, core: 2. Of those that a mesh axis runs over, the one named last changes fastest.
Arguments:
- x_raw: bfloat16 [4096, 4096], P('seq', 'head'), may hold values from -6 to 6
- bc_raw: bfloat16 [4096, 256], P('seq'), may hold values from -6 to 6
- dt_raw: float32 [4096, 64], P('seq', 'head')
- conv_x: float32 [4, 4096], P(None, 'head'), may hold values from -3 to 3
- conv_bc: float32 [4, 256], replicated, may hold values from -3 to 3
- dt_bias: float32 [64], P('head')
- a_log: float32 [64], P('head'), may hold values from 0 to 2.1
- skip_d: float32 [64], P('head'), may hold values from 0.5 to 2
- d_out: bfloat16 [4096, 4096], P('seq', 'head'), may hold values from -6 to 6
Outputs:
- layer_out: bfloat16 [4096, 4096], P('seq', 'head')
- grad_x: bfloat16 [4096, 4096], P('seq', 'head')
- grad_bc: float32 [4096, 256], P('seq')
- grad_steps: float32 [4096, 64], P('seq', 'head')
- grad_conv_x: float32 [4, 4096], P(None, 'head')
- grad_conv_bc: float32 [4, 256], replicated
- grad_bias: float32 [64], P('head')
- grad_rates: float32 [64], P('head')
- grad_skip: float32 [64], P('head')
The draws below stay inside these ranges and needn't reach their ends.
All inputs are finite; a program needn't handle non-finite values.
Results may differ from the reference program's by a relative error of at most 0.001.
Values may be sent and summed in bfloat16 or wider, within the bound.
A program may use at most 128 MiB of HBM per device.

```python
import math
import jax
import jax.numpy as jnp
from jax import lax

NH = 64
P_SIZE = 64
N = 128
BLOCK = 128
KW = 4
L_DEV = 512
DI = 4096
SEQ = 4096
N_SEQ = 8
N_HEAD = 4


def head_rates(key, share):
    key_mag, key_slow, key_slow_rate, key_fast_rate = jax.random.split(jax.random.fold_in(key, 11), 4)
    magnitude = jnp.exp(jax.random.uniform(key_mag, (NH,), jnp.float32, 0.0, math.log(8.0)))
    slow = jax.random.uniform(key_slow, (NH,), jnp.float32) < share
    slow_rate = jax.random.uniform(key_slow_rate, (NH,), jnp.float32, 0.4, 1.6) / SEQ
    fast_rate = jax.random.uniform(key_fast_rate, (NH,), jnp.float32, 1.0 / 50.0, 1.0 / 25.0)
    per_step = jnp.where(slow, slow_rate, fast_rate)
    return (jnp.log(magnitude), jnp.log(jnp.expm1(per_step / magnitude)))


def draw_a_log(key, part):
    share = 0.5
    return head_rates(key, share)[0]


def draw_dt_bias(key, part):
    share = 0.5
    return head_rates(key, share)[1]


def draw_dt_raw(key, part):
    key_noise, key_where = jax.random.split(jax.random.fold_in(key, 23))
    noise = jnp.clip(0.5 * jax.random.normal(key_noise, (SEQ, NH), jnp.float32), -3.0, 3.0)
    places = jax.random.randint(key_where, (8,), 0, SEQ)
    frames = jnp.arange(SEQ)
    struck = jnp.any(frames[:, None] == places[None, :], axis=1)
    boost = jnp.where(struck, math.log(SEQ) - 1.5, 0.0).astype(jnp.float32)
    return noise + boost[:, None]


def levels(own_key, shape, shards, least, largest):
    level = 1.0
    for dim, blocks in shards:
        heights = jax.random.uniform(jax.random.fold_in(jax.random.fold_in(own_key, 6), dim), (blocks,), jnp.float32, least / len(shards), largest / len(shards))
        level = level * jnp.repeat(jnp.exp(heights), shape[dim] // blocks).reshape((-1,) + (1,) * (len(shape) - 1 - dim))
    return level


def gaussian(own_key, dims, scale, limit, shards=(), kind=jnp.bfloat16):
    entries = scale * jax.random.normal(own_key, dims, jnp.float32)
    if shards:
        entries = entries * levels(own_key, dims, shards, -0.22, 0.18)
    return jnp.clip(entries, -limit, limit).astype(kind)


def setup_inputs(seed: int = 0) -> dict:
    keys = jax.random.split(jax.random.key(seed), 10)
    x_raw = gaussian(keys[0], (SEQ, DI), 1.0, 6.0, ((0, 8), (1, 4)))
    bc_raw = gaussian(keys[1], (SEQ, 2 * N), 1.0, 6.0, ((0, 8),))
    dt_raw = draw_dt_raw(jax.random.fold_in(keys[9], 71), 0)
    conv_x = gaussian(keys[3], (KW, DI), KW ** -0.5, 3.0, ((1, 4),), jnp.float32)
    conv_bc = gaussian(keys[4], (KW, 2 * N), KW ** -0.5, 3.0, (), jnp.float32)
    dt_bias = draw_dt_bias(jax.random.fold_in(keys[9], 71), 0)
    a_log = draw_a_log(jax.random.fold_in(keys[9], 71), 0)
    skip_d = jnp.clip(0.5 + 1.5 * jax.random.uniform(keys[7], (NH,), jnp.float32) ** levels(keys[7], (NH,), ((0, 4),), -0.2, 0.2), 0.5, 2.0)
    d_out = gaussian(keys[8], (SEQ, DI), 1.0, 6.0, ((0, 8), (1, 4)))
    return dict(x_raw=x_raw, bc_raw=bc_raw, dt_raw=dt_raw, conv_x=conv_x, conv_bc=conv_bc, dt_bias=dt_bias, a_log=a_log, skip_d=skip_d, d_out=d_out)


def conv_pre(padded, taps):
    frames = padded.shape[0] - taps.shape[0] + 1
    total = taps[0] * padded[0:frames].astype(jnp.float32)
    for offset in range(1, taps.shape[0]):
        total = total + taps[offset] * padded[offset:offset + frames].astype(jnp.float32)
    return total

def block_terms(x_act, b_proj, step_size, log_decay):
    frames, width = x_act.shape
    head_count = step_size.shape[1]
    num_blocks = frames // BLOCK
    running = jnp.cumsum(log_decay.reshape(num_blocks, BLOCK, head_count), axis=1)
    to_end = jnp.exp(running[:, -1:, :] - running)
    scaled = x_act.reshape(num_blocks, BLOCK, head_count, width // head_count) * (step_size.reshape(num_blocks, BLOCK, head_count) * to_end)[..., None]
    block_states = jnp.einsum('kqn,kqhp->khpn', b_proj.reshape(num_blocks, BLOCK, -1), scaled, precision=lax.Precision.HIGHEST)
    return (running, block_states)

def block_mix(block_states, running, state_in):
    block_log = running[:, -1, :]
    totals = jnp.concatenate([jnp.zeros((1, block_log.shape[1]), jnp.float32), jnp.cumsum(block_log, axis=0)], axis=0)
    count = totals.shape[0]
    later = jnp.arange(count)[:, None] >= jnp.arange(count)[None, :]
    log_gaps = totals[:, None, :] - totals[None, :, :]
    decay_mat = jnp.exp(jnp.where(later[:, :, None], log_gaps, -jnp.inf))
    stacked = jnp.concatenate([state_in[None], block_states], axis=0)
    mixed = jnp.einsum('zch,chpn->zhpn', decay_mat, stacked, precision=lax.Precision.HIGHEST)
    return (mixed[:-1], mixed[-1], totals)

def emit(x_act, b_proj, c_proj, step_size, running, block_states, skip_d, state_in):
    frames, width = x_act.shape
    head_count = step_size.shape[1]
    num_blocks = frames // BLOCK
    state_heads, state_out, totals = block_mix(block_states, running, state_in)
    x_blocks = x_act.reshape(num_blocks, BLOCK, head_count, width // head_count)
    b_blocks = b_proj.reshape(num_blocks, BLOCK, -1)
    c_blocks = c_proj.reshape(num_blocks, BLOCK, -1)
    step_blocks = step_size.reshape(num_blocks, BLOCK, head_count)
    scores = jnp.einsum('kin,kjn->kij', c_blocks, b_blocks, precision=lax.Precision.HIGHEST)
    causal = jnp.arange(BLOCK)[:, None] >= jnp.arange(BLOCK)[None, :]
    log_gaps = running[:, :, None, :] - running[:, None, :, :]
    decay_mat = jnp.exp(jnp.where(causal[None, :, :, None], log_gaps, -jnp.inf))
    weights = scores[..., None] * decay_mat * step_blocks[:, None, :, :]
    y_diag = jnp.einsum('kijh,kjhp->kihp', weights, x_blocks, precision=lax.Precision.HIGHEST)
    y_carry = jnp.einsum('kin,khpn->kihp', c_blocks, state_heads, precision=lax.Precision.HIGHEST) * jnp.exp(running)[..., None]
    y_full = y_diag + y_carry + skip_d[None, None, :, None] * x_blocks
    return (y_full.reshape(frames, width), state_out)

def forward(x_raw, bc_raw, dt_raw, conv_x, conv_bc, dt_bias, a_log, skip_d):
    margin = KW - 1
    bc_act = jax.nn.silu(conv_pre(jnp.pad(bc_raw, ((margin, 0), (0, 0))), conv_bc))
    b_proj = bc_act[:, :N]
    c_proj = bc_act[:, N:]
    head_count = NH // N_HEAD
    width = head_count * P_SIZE

    def head_group(index):
        start = (index * width).astype(jnp.int32)
        first = (index * head_count).astype(jnp.int32)
        x_part = lax.dynamic_slice_in_dim(x_raw, start, width, 1)
        taps = lax.dynamic_slice_in_dim(conv_x, start, width, 1)
        raw_steps = lax.dynamic_slice_in_dim(dt_raw, first, head_count, 1)
        biases = lax.dynamic_slice_in_dim(dt_bias, first, head_count, 0)
        rate_logs = lax.dynamic_slice_in_dim(a_log, first, head_count, 0)
        skips = lax.dynamic_slice_in_dim(skip_d, first, head_count, 0)
        x_act = jax.nn.silu(conv_pre(jnp.pad(x_part, ((margin, 0), (0, 0))), taps))
        step_size = jax.nn.softplus(raw_steps + biases)
        log_decay = -step_size * jnp.exp(rate_logs)

        def advance(state, pieces):
            x_blk, b_blk, c_blk, step_blk, log_blk = pieces
            running, block_states = block_terms(x_blk, b_blk, step_blk, log_blk)
            y_blk, state_out = emit(x_blk, b_blk, c_blk, step_blk, running, block_states, skips, state)
            return (state_out, y_blk)
        inputs = (x_act.reshape(N_SEQ, L_DEV, width), b_proj.reshape(N_SEQ, L_DEV, N), c_proj.reshape(N_SEQ, L_DEV, N), step_size.reshape(N_SEQ, L_DEV, head_count), log_decay.reshape(N_SEQ, L_DEV, head_count))
        _, outputs = lax.scan(advance, jnp.zeros((head_count, P_SIZE, N), jnp.float32), inputs)
        return outputs.reshape(SEQ, width)
    per_group = lax.map(jax.checkpoint(head_group), jnp.arange(N_HEAD, dtype=jnp.int32))
    return jnp.transpose(per_group, (1, 0, 2)).reshape(SEQ, NH * P_SIZE)

def reference(x_raw, bc_raw, dt_raw, conv_x, conv_bc, dt_bias, a_log, skip_d, d_out):
    y_full, pullback = jax.vjp(forward, x_raw.astype(jnp.float32), bc_raw.astype(jnp.float32), dt_raw, conv_x, conv_bc, dt_bias, a_log, skip_d)
    grads = pullback(d_out.astype(jnp.float32))
    return (y_full.astype(jnp.bfloat16), grads[0].astype(jnp.bfloat16), grads[1], grads[2], grads[3], grads[4], grads[5], grads[6], grads[7])
```

```python
import jax
import jax.numpy as jnp
from jax import lax
from jax.experimental import pallas as pl
from jax.experimental.pallas import tpu as pltpu
from jax.sharding import PartitionSpec as P

P_SIZE = 64
N = 128
BLOCK = 128
LANES = 128
F32 = jnp.float32
BF16 = jnp.bfloat16
NN = (((1,), (0,)), ((), ()))
NT = (((1,), (1,)), ((), ()))
TN = (((0,), (0,)), ((), ()))
MESH = pl.DeviceIdType.MESH
VMEM_LIMIT = 44 * 2**20


def shifted(block, axis, distance):
    devices = range(lax.axis_size(axis))
    route = [(i - distance, i) for i in devices if i - distance in devices]
    return lax.ppermute(block, axis, route)


def split(a):
    high = a.astype(BF16)
    return high, (a - high.astype(F32)).astype(BF16)


def mm(a, b, dims=NN):
    return lax.dot_general(a, b, dims, preferred_element_type=F32)


def dot3(a, b, dims=NN):
    return mm(a[0], b[0], dims) + (mm(a[0], b[1], dims) + mm(a[1], b[0], dims))


def exact(a, b, dims=NN):
    return lax.dot_general(
        a, b, dims, precision=lax.Precision.HIGHEST, preferred_element_type=F32
    )


def silu(pre):
    return pre / (1.0 + jnp.exp(-pre))


def lane_ids(shape):
    return lax.broadcasted_iota(jnp.int32, shape, 1)


def row_ids(shape):
    return lax.broadcasted_iota(jnp.int32, shape, 0)


def rows_of(k):
    return slice(k * BLOCK, (k + 1) * BLOCK)


def pair_columns(rolled):
    first = jnp.broadcast_to(rolled[:, 0:1], rolled.shape)
    second = jnp.broadcast_to(rolled[:, 1:2], rolled.shape)
    return jnp.where(lane_ids(rolled.shape) < P_SIZE, first, second)


def conv_x_pre(xp, halo_ref, x_ref, taps_ref):
    frames = x_ref.shape[0]
    xp[0:8, :] = halo_ref[...]
    xp[8 : 8 + frames, :] = x_ref[...].astype(F32)
    pre = taps_ref[0:1, :] * xp[5 : 5 + frames, :]
    for k in range(1, 4):
        pre = pre + taps_ref[k : k + 1, :] * xp[5 + k : 5 + k + frames, :]
    return pre


def terms_kernel(
    halo_ref, x_ref, gy_ref, taps_ref, bc_ref, taps_bc_ref, s_ref, la_ref,
    bs_ref, bg_ref, ls_ref, lg_ref, dec_ref, run_ref, b_ref, c_ref, sc_ref, runt_ref,
    xp, bth, btl, cth, ctl,
):
    p = pl.program_id(0)
    frames = x_ref.shape[0]
    blocks = frames // BLOCK

    @pl.when(p == 0)
    def _():
        square = (BLOCK, BLOCK)
        tril = jnp.where(row_ids(square) >= lane_ids(square), 1.0, 0.0).astype(F32)
        pre = taps_bc_ref[0:1, :] * bc_ref[5 : 5 + frames, :]
        for k in range(1, 4):
            pre = pre + taps_bc_ref[k : k + 1, :] * bc_ref[5 + k : 5 + k + frames, :]
        act = silu(pre)
        b_ref[...] = act[:, :N]
        c_ref[...] = act[:, N:]
        for k in range(blocks):
            run = exact(tril, la_ref[rows_of(k), :])
            run_ref[rows_of(k), :] = run
            runt_ref[k] = run.T
            b = b_ref[rows_of(k), :]
            c = c_ref[rows_of(k), :]
            bth[k], btl[k] = split(b.T)
            cth[k], ctl[k] = split(c.T)
            sc_ref[k] = exact(c, b, NT)

    xa = silu(conv_x_pre(xp, halo_ref, x_ref, taps_ref))
    back = lax.rem(LANES - 2 * p, LANES)
    state = jnp.zeros((N, LANES), F32)
    total = jnp.zeros((1, LANES), F32)
    decays = []
    for k in range(blocks):
        run = pair_columns(pltpu.roll(run_ref[rows_of(k), :], back, 1))
        step = pair_columns(pltpu.roll(s_ref[rows_of(k), :], back, 1))
        tot = run[BLOCK - 1 : BLOCK, :]
        scaled = xa[rows_of(k), :] * (step * jnp.exp(tot - run))
        bs = dot3((bth[k], btl[k]), split(scaled))
        bs_ref[0, k] = bs
        bg_ref[0, k] = dot3(
            (cth[k], ctl[k]), split(gy_ref[rows_of(k), :].astype(F32) * jnp.exp(run))
        )
        decays.append(jnp.exp(tot))
        state = decays[k] * state + bs
        total = total + tot
    ls_ref[0] = state
    grad = jnp.zeros((N, LANES), F32)
    for k in reversed(range(blocks)):
        grad = decays[k] * grad + bg_ref[0, k]
    lg_ref[0] = grad
    dec_ref[0] = jnp.broadcast_to(jnp.exp(total), (8, LANES))


def chain_kernel(
    size, ls_ref, lg_ref, dec_ref, sin_ref, gin_ref,
    fout, fin, bout, bin_, fsend, frecv, bsend, brecv,
):
    me = lax.axis_index("seq")
    chunks = ls_ref.shape[0]
    lag = 2
    barrier = pltpu.get_barrier_semaphore()

    @pl.when(me > 0)
    def _():
        pl.semaphore_signal(barrier, inc=1, device_id={"seq": me - 1}, device_id_type=MESH)

    @pl.when(me < size - 1)
    def _():
        pl.semaphore_signal(barrier, inc=1, device_id={"seq": me + 1}, device_id_type=MESH)

    pl.semaphore_wait(barrier, lax.min(me, 1) + lax.min(size - 1 - me, 1))

    def copy(out, into, send, recv, k, target):
        return pltpu.make_async_remote_copy(
            src_ref=out.at[k],
            dst_ref=into.at[k],
            send_sem=send.at[k],
            recv_sem=recv.at[k],
            device_id={"seq": target},
            device_id_type=MESH,
        )

    def forward(k):
        @pl.when(me == 0)
        def _():
            sin_ref[k] = jnp.zeros((N, LANES), F32)
            fout[k] = ls_ref[k]

        @pl.when(me > 0)
        def _():
            copy(fout, fin, fsend, frecv, k, me - 1).wait_recv()
            got = fin[k]
            sin_ref[k] = got
            fout[k] = dec_ref[k][0:1, :] * got + ls_ref[k]

        @pl.when(me < size - 1)
        def _():
            copy(fout, fin, fsend, frecv, k, me + 1).start()

    def backward(k):
        @pl.when(me == size - 1)
        def _():
            gin_ref[k] = jnp.zeros((N, LANES), F32)
            bout[k] = lg_ref[k]

        @pl.when(me < size - 1)
        def _():
            copy(bout, bin_, bsend, brecv, k, me + 1).wait_recv()
            got = bin_[k]
            gin_ref[k] = got
            bout[k] = dec_ref[k][0:1, :] * got + lg_ref[k]

        @pl.when(me > 0)
        def _():
            copy(bout, bin_, bsend, brecv, k, me - 1).start()

    late_f = lax.max(0, 2 * me - (size - 1)) * lag
    late_b = lax.max(0, (size - 1) - 2 * me) * lag

    def turn(step, carry):
        kf = step - late_f
        kb = step - late_b

        @pl.when(jnp.logical_and(kf >= 0, kf < chunks))
        def _():
            forward(kf)

        @pl.when(jnp.logical_and(kb >= 0, kb < chunks))
        def _():
            backward(kb)

        return carry

    lax.fori_loop(0, chunks + (size - 1) * lag, turn, 0)

    def drain(k, carry):
        @pl.when(me < size - 1)
        def _():
            copy(fout, fin, fsend, frecv, k, me + 1).wait_send()

        @pl.when(me > 0)
        def _():
            copy(bout, bin_, bsend, brecv, k, me - 1).wait_send()

        return carry

    lax.fori_loop(0, chunks, drain, 0)


def main_kernel(
    halo_ref, x_ref, gy_ref, taps_ref, skip_ref, s_ref, run_ref, runt_ref,
    b_ref, c_ref, sc_ref, bs_ref, bg_ref, sin_ref, gin_ref,
    out_ref, gx_ref, tail_ref, first_ref, tapg_ref, skipg_ref, dbc_ref, u_ref, v_ref, bnd_ref,
    xp, gp, zs, gs, bh, bl, ch, cl,
):
    p = pl.program_id(0)
    frames = x_ref.shape[0]
    blocks = frames // BLOCK
    square = (BLOCK, BLOCK)

    @pl.when(p == 0)
    def _():
        bh[...], bl[...] = split(b_ref[...])
        ch[...], cl[...] = split(c_ref[...])
        gs[...] = jnp.zeros_like(gs)
        dbc_ref[...] = jnp.zeros_like(dbc_ref)
        u_ref[...] = jnp.zeros_like(u_ref)
        v_ref[...] = jnp.zeros_like(v_ref)
        bnd_ref[...] = jnp.zeros_like(bnd_ref)

    pre = conv_x_pre(xp, halo_ref, x_ref, taps_ref)
    gate = 1.0 / (1.0 + jnp.exp(-pre))
    xa = pre * gate
    slope = gate * (1.0 + pre * (1.0 - gate))
    back = lax.rem(LANES - 2 * p, LANES)
    causal = row_ids(square) >= lane_ids(square)
    low = lane_ids(square) < P_SIZE
    heads = jnp.where(
        lane_ids(square) == 2 * p + row_ids(square) // P_SIZE, 1.0, 0.0
    ).astype(BF16)
    nothing = jnp.zeros(square, BF16)

    runs = []
    decays = []
    for k in range(blocks):
        rolled = pltpu.roll(run_ref[rows_of(k), :], back, 1)
        runs.append(rolled)
        wide = pair_columns(rolled[BLOCK - 8 : BLOCK, :])
        decays.append(jnp.exp(wide[7:8, :]))
    grads = [None] * blocks
    grad = gin_ref[0]
    for k in reversed(range(blocks)):
        grads[k] = grad
        grad = decays[k] * grad + bg_ref[0, k]

    state = sin_ref[0]
    for k in range(blocks):
        rows = rows_of(k)
        x = xa[rows, :]
        gyh = gy_ref[rows, :]
        gy = gyh.astype(F32)
        run = pair_columns(runs[k])
        step = pair_columns(pltpu.roll(s_ref[rows, :], back, 1))
        reach = jnp.exp(run)
        to_end = jnp.exp(run[BLOCK - 1 : BLOCK, :] - run)
        xs = x * step
        xsh, xsl = split(xs)
        stored = split(state)
        graded = split(grads[k])
        b2 = (bh[rows, :], bl[rows, :])
        c2 = (ch[rows, :], cl[rows, :])
        gy_heads = jnp.concatenate(
            [jnp.where(low, gyh, nothing), jnp.where(low, nothing, gyh)], axis=0
        )
        prod = mm(gy_heads, xsh, NT) + mm(gy_heads, xsl, NT)
        weights = []
        score_grad = gs[k]
        for half in range(2):
            gap = runs[k][:, half : half + 1] - runt_ref[k, pl.ds(2 * p + half, 1), :]
            decay = jnp.exp(jnp.where(causal, gap, -jnp.inf))
            weights.append(split(sc_ref[k] * decay))
            score_grad = score_grad + decay * prod[half * BLOCK : (half + 1) * BLOCK, :]
        gs[k] = score_grad
        wh = jnp.concatenate([weights[0][0], weights[1][0]], axis=1)
        wl = jnp.concatenate([weights[0][1], weights[1][1]], axis=1)
        xh2 = jnp.concatenate(
            [jnp.where(low, xsh, nothing), jnp.where(low, nothing, xsh)], axis=0
        )
        xl2 = jnp.concatenate(
            [jnp.where(low, xsl, nothing), jnp.where(low, nothing, xsl)], axis=0
        )
        y_scan = mm(wh, xh2) + (mm(wh, xl2) + mm(wl, xh2)) + reach * dot3(c2, stored)
        tall_h = jnp.concatenate([weights[0][0], weights[1][0]], axis=0)
        tall_l = jnp.concatenate([weights[0][1], weights[1][1]], axis=0)
        z = mm(tall_h, gy_heads, TN) + mm(tall_l, gy_heads, TN) + to_end * dot3(b2, graded)
        out_ref[rows, :] = (y_scan + skip_ref[0:1, :] * x).astype(BF16)
        zs[rows, :] = z * step + skip_ref[0:1, :] * gy
        u2 = split(gy * y_scan)
        v2 = split(x * z)
        u_ref[rows, :] += mm(u2[0], heads) + mm(u2[1], heads)
        v_ref[rows, :] += mm(v2[0], heads) + mm(v2[1], heads)
        dbc_ref[rows, :N] += dot3(split(xs * to_end), graded, NT)
        dbc_ref[rows, N:] += dot3(split(gy * reach), stored, NT)
        state = decays[k] * state + bs_ref[0, k]
        crossing = jnp.broadcast_to(jnp.sum(state * grads[k], axis=0, keepdims=True), (8, LANES))
        cross2 = split(crossing)
        bnd_ref[k] += mm(cross2[0], heads) + mm(cross2[1], heads)

    skipg_ref[...] = jnp.broadcast_to(
        jnp.sum(xa * gy_ref[...].astype(F32), axis=0, keepdims=True), (8, LANES)
    )
    g = zs[...] * slope
    gp[0:frames, :] = g
    gp[frames : frames + 8, :] = jnp.zeros((8, LANES), F32)
    gx = taps_ref[0:1, :] * gp[3 : 3 + frames, :]
    for k in range(1, 4):
        gx = gx + taps_ref[k : k + 1, :] * gp[3 - k : 3 - k + frames, :]
    gx_ref[...] = gx.astype(BF16)
    tail_ref[...] = gx[frames - 8 :, :]
    first_ref[...] = g[0:8, :]
    for k in range(4):
        tapg_ref[k : k + 1, :] = jnp.sum(
            g * xp[5 + k : 5 + k + frames, :], axis=0, keepdims=True
        )

    @pl.when(p == pl.num_programs(0) - 1)
    def _():
        for k in range(blocks):
            rows = rows_of(k)
            gk = split(gs[k])
            gt = split(gs[k].T)
            dbc_ref[rows, :N] += dot3(gt, (ch[rows, :], cl[rows, :]))
            dbc_ref[rows, N:] += dot3(gk, (bh[rows, :], bl[rows, :]))


def local(x_raw, bc_raw, dt_raw, conv_x, conv_bc, dt_bias, a_log, skip_d, d_out):
    margin = conv_x.shape[0] - 1
    frames, width = x_raw.shape
    head_count = dt_raw.shape[1]
    blocks = frames // BLOCK
    pairs = width // LANES
    size = lax.axis_size("seq")
    shape = jax.ShapeDtypeStruct

    tails = jnp.concatenate([x_raw[-margin:], bc_raw[-margin:]], axis=1)
    before = shifted(tails, "seq", 1)
    halo = jnp.pad(before.astype(F32), ((8 - margin, 0), (0, 0)))
    x_halo = halo[:, :width]
    bc_ext = jnp.concatenate([halo[:, width:], bc_raw.astype(F32)], axis=0)
    raw_sum = dt_raw + dt_bias
    step_size = jax.nn.softplus(raw_sum)
    rates = jnp.exp(a_log)
    log_decay = -step_size * rates
    padding = ((0, 0), (0, LANES - head_count))
    s_pad = jnp.pad(step_size, padding)
    la_pad = jnp.pad(log_decay, padding)
    skip_wide = jnp.broadcast_to(jnp.repeat(skip_d, P_SIZE)[None], (8, width))

    def whole(*dims):
        return pl.BlockSpec(dims, lambda p: (0,) * len(dims))

    def columns(rows):
        return pl.BlockSpec((rows, LANES), lambda p: (0, p))

    def pair(*dims):
        return pl.BlockSpec((1,) + dims, lambda p: (p,) + (0,) * len(dims))

    bs, bg, ls, lg, dec, run, b_act, c_act, scores, runt = pl.pallas_call(
        terms_kernel,
        grid=(pairs,),
        in_specs=[
            columns(8), columns(frames), columns(frames), columns(4),
            whole(frames + 8, 2 * N), whole(4, 2 * N), whole(frames, LANES), whole(frames, LANES),
        ],
        out_specs=[
            pair(blocks, N, LANES), pair(blocks, N, LANES), pair(N, LANES), pair(N, LANES),
            pair(8, LANES), whole(frames, LANES), whole(frames, N), whole(frames, N),
            whole(blocks, BLOCK, BLOCK), whole(blocks, LANES, BLOCK),
        ],
        out_shape=[
            shape((pairs, blocks, N, LANES), F32), shape((pairs, blocks, N, LANES), F32),
            shape((pairs, N, LANES), F32), shape((pairs, N, LANES), F32),
            shape((pairs, 8, LANES), F32), shape((frames, LANES), F32),
            shape((frames, N), F32), shape((frames, N), F32),
            shape((blocks, BLOCK, BLOCK), F32), shape((blocks, LANES, BLOCK), F32),
        ],
        scratch_shapes=[pltpu.VMEM((frames + 8, LANES), F32)]
        + [pltpu.VMEM((blocks, N, BLOCK), BF16)] * 4,
        compiler_params=pltpu.CompilerParams(vmem_limit_bytes=VMEM_LIMIT),
        name="terms",
    )(x_halo, x_raw, d_out, conv_x, bc_ext, conv_bc, s_pad, la_pad)

    in_vmem = pl.BlockSpec(memory_space=pltpu.VMEM)
    state_in, grad_in = pl.pallas_call(
        lambda *refs: chain_kernel(size, *refs),
        in_specs=[in_vmem] * 3,
        out_specs=[in_vmem] * 2,
        out_shape=[shape((pairs, N, LANES), F32)] * 2,
        scratch_shapes=[pltpu.VMEM((pairs, N, LANES), F32)] * 4
        + [pltpu.SemaphoreType.DMA((pairs,))] * 4,
        compiler_params=pltpu.CompilerParams(
            collective_id=0, has_side_effects=True, vmem_limit_bytes=VMEM_LIMIT
        ),
        name="chain",
    )(ls, lg, dec)

    layer_out, grad_x, tail, first, tap_grad, skip_grad, bc_local, u, v, bnd = pl.pallas_call(
        main_kernel,
        grid=(pairs,),
        in_specs=[
            columns(8), columns(frames), columns(frames), columns(4), columns(8),
            whole(frames, LANES), whole(frames, LANES), whole(blocks, LANES, BLOCK),
            whole(frames, N), whole(frames, N), whole(blocks, BLOCK, BLOCK),
            pair(blocks, N, LANES), pair(blocks, N, LANES), pair(N, LANES), pair(N, LANES),
        ],
        out_specs=[
            columns(frames), columns(frames), columns(8), columns(8), columns(4), columns(8),
            whole(frames, 2 * N), whole(frames, LANES), whole(frames, LANES),
            whole(blocks, 8, LANES),
        ],
        out_shape=[
            shape((frames, width), BF16), shape((frames, width), BF16),
            shape((8, width), F32), shape((8, width), F32), shape((4, width), F32),
            shape((8, width), F32), shape((frames, 2 * N), F32),
            shape((frames, LANES), F32), shape((frames, LANES), F32),
            shape((blocks, 8, LANES), F32),
        ],
        scratch_shapes=[
            pltpu.VMEM((frames + 8, LANES), F32), pltpu.VMEM((frames + 8, LANES), F32),
            pltpu.VMEM((frames, LANES), F32), pltpu.VMEM((blocks, BLOCK, BLOCK), F32),
        ]
        + [pltpu.VMEM((frames, N), BF16)] * 4,
        compiler_params=pltpu.CompilerParams(vmem_limit_bytes=VMEM_LIMIT),
        name="main",
    )(
        x_halo, x_raw, d_out, conv_x, skip_wide, s_pad, run, runt,
        b_act, c_act, scores, bs, bg, state_in, grad_in,
    )

    bc_pre = conv_bc[0] * bc_ext[5 : 5 + frames]
    for k in range(1, 4):
        bc_pre = bc_pre + conv_bc[k] * bc_ext[5 + k : 5 + k + frames]
    gate = jax.nn.sigmoid(bc_pre)
    bc_grad = lax.psum(bc_local, "head") * (gate * (1.0 + bc_pre * (1.0 - gate)))
    conv_bc_grad = jnp.stack(
        [jnp.sum(bc_grad * bc_ext[5 + k : 5 + k + frames], axis=0) for k in range(4)]
    )
    after = shifted(jnp.concatenate([first[:margin], bc_grad[:margin]], axis=1), "seq", -1)
    bc_spread = jnp.concatenate([bc_grad, after[:, width:]], axis=0)
    grad_bc = conv_bc[0] * bc_spread[3 : 3 + frames]
    for k in range(1, 4):
        grad_bc = grad_bc + conv_bc[k] * bc_spread[3 - k : 3 - k + frames]
    x_after = jnp.pad(after[:, :width], ((margin, 0), (0, 0)))
    patch = tail[8 - margin :]
    for k in range(margin):
        patch = patch + conv_x[k] * x_after[3 - k : 6 - k]
    grad_x = lax.dynamic_update_slice(grad_x, patch.astype(BF16), (frames - margin, 0))

    u = u[:, :head_count]
    v = v[:, :head_count]
    net = (u - step_size * v).reshape(blocks, BLOCK, head_count)
    upper = (jnp.arange(BLOCK)[:, None] <= jnp.arange(BLOCK)[None, :]).astype(F32)
    g_log = jnp.einsum("tq,kqh->kth", upper, net, precision=lax.Precision.HIGHEST)
    g_log = (g_log + bnd[:, 0:1, :head_count]).reshape(frames, head_count)
    grad_steps = (v - g_log * rates) * jax.nn.sigmoid(raw_sum)
    skip_part = jnp.sum(skip_grad[0].reshape(head_count, P_SIZE), axis=1)
    summed = lax.psum(
        jnp.concatenate(
            [
                tap_grad.reshape(-1),
                conv_bc_grad.reshape(-1),
                jnp.sum(grad_steps, axis=0),
                jnp.sum(g_log * log_decay, axis=0),
                skip_part,
            ]
        ),
        "seq",
    )
    cuts = [4 * width, 8 * N, head_count, head_count, head_count]
    parts = []
    at = 0
    for cut in cuts:
        parts.append(summed[at : at + cut])
        at += cut
    return (
        layer_out,
        grad_x,
        grad_bc,
        grad_steps,
        parts[0].reshape(4, width),
        parts[1].reshape(4, 2 * N),
        parts[2],
        parts[3],
        parts[4],
    )


def solution(mesh):
    placed = (
        P("seq", "head"),
        P("seq", None),
        P("seq", "head"),
        P(None, "head"),
        P(),
        P("head"),
        P("head"),
        P("head"),
        P("seq", "head"),
    )
    return jax.shard_map(
        local,
        mesh=mesh,
        in_specs=placed,
        out_specs=(
            P("seq", "head"),
            P("seq", "head"),
            P("seq", None),
            P("seq", "head"),
            P(None, "head"),
            P(),
            P("head"),
            P("head"),
            P("head"),
        ),
        check_vma=False,
    )
```

```python
import jax
import jax.numpy as jnp
from jax import lax
from jax.experimental import pallas as pl
from jax.experimental.pallas import tpu as pltpu
from jax.sharding import PartitionSpec as P

P_SIZE = 64
N = 128
BLOCK = 128
LANES = 128
F32 = jnp.float32
BF16 = jnp.bfloat16
NN = (((1,), (0,)), ((), ()))
NT = (((1,), (1,)), ((), ()))
TN = (((0,), (0,)), ((), ()))
MESH = pl.DeviceIdType.MESH
VMEM_LIMIT = 44 * 2**20


def shifted(block, axis, distance):
    devices = range(lax.axis_size(axis))
    route = [(i - distance, i) for i in devices if i - distance in devices]
    return lax.ppermute(block, axis, route)


def split(a):
    high = a.astype(BF16)
    return high, (a - high.astype(F32)).astype(BF16)


def mm(a, b, dims=NN):
    return lax.dot_general(a, b, dims, preferred_element_type=F32)


def dot3(a, b, dims=NN):
    return mm(a[0], b[0], dims) + (mm(a[0], b[1], dims) + mm(a[1], b[0], dims))


def exact(a, b, dims=NN):
    return lax.dot_general(
        a, b, dims, precision=lax.Precision.HIGHEST, preferred_element_type=F32
    )


def silu(pre):
    return pre / (1.0 + jnp.exp(-pre))


def lane_ids(shape):
    return lax.broadcasted_iota(jnp.int32, shape, 1)


def row_ids(shape):
    return lax.broadcasted_iota(jnp.int32, shape, 0)


def rows_of(k):
    return slice(k * BLOCK, (k + 1) * BLOCK)


def pair_columns(rolled):
    first = jnp.broadcast_to(rolled[:, 0:1], rolled.shape)
    second = jnp.broadcast_to(rolled[:, 1:2], rolled.shape)
    return jnp.where(lane_ids(rolled.shape) < P_SIZE, first, second)


def conv_x_pre(xp, halo_ref, x_ref, taps_ref):
    frames = x_ref.shape[0]
    xp[0:8, :] = halo_ref[...]
    xp[8 : 8 + frames, :] = x_ref[...].astype(F32)
    pre = taps_ref[0:1, :] * xp[5 : 5 + frames, :]
    for k in range(1, 4):
        pre = pre + taps_ref[k : k + 1, :] * xp[5 + k : 5 + k + frames, :]
    return pre


def terms_kernel(
    halo_ref, x_ref, gy_ref, taps_ref, bc_ref, taps_bc_ref, s_ref, la_ref,
    bs_ref, bg_ref, ls_ref, lg_ref, dec_ref, run_ref, b_ref, c_ref, sc_ref, runt_ref,
    xp, bth, btl, cth, ctl,
):
    p = pl.program_id(0)
    frames = x_ref.shape[0]
    blocks = frames // BLOCK

    @pl.when(p == 0)
    def _():
        square = (BLOCK, BLOCK)
        tril = jnp.where(row_ids(square) >= lane_ids(square), 1.0, 0.0).astype(F32)
        pre = taps_bc_ref[0:1, :] * bc_ref[5 : 5 + frames, :]
        for k in range(1, 4):
            pre = pre + taps_bc_ref[k : k + 1, :] * bc_ref[5 + k : 5 + k + frames, :]
        act = silu(pre)
        b_ref[...] = act[:, :N]
        c_ref[...] = act[:, N:]
        for k in range(blocks):
            run = exact(tril, la_ref[rows_of(k), :])
            run_ref[rows_of(k), :] = run
            runt_ref[k] = run.T
            b = b_ref[rows_of(k), :]
            c = c_ref[rows_of(k), :]
            bth[k], btl[k] = split(b.T)
            cth[k], ctl[k] = split(c.T)
            sc_ref[k] = exact(c, b, NT)

    xa = silu(conv_x_pre(xp, halo_ref, x_ref, taps_ref))
    back = lax.rem(LANES - 2 * p, LANES)
    state = jnp.zeros((N, LANES), F32)
    total = jnp.zeros((1, LANES), F32)
    decays = []
    for k in range(blocks):
        run = pair_columns(pltpu.roll(run_ref[rows_of(k), :], back, 1))
        step = pair_columns(pltpu.roll(s_ref[rows_of(k), :], back, 1))
        tot = run[BLOCK - 1 : BLOCK, :]
        scaled = xa[rows_of(k), :] * (step * jnp.exp(tot - run))
        bs = dot3((bth[k], btl[k]), split(scaled))
        bs_ref[0, k] = bs
        bg_ref[0, k] = dot3(
            (cth[k], ctl[k]), split(gy_ref[rows_of(k), :].astype(F32) * jnp.exp(run))
        )
        decays.append(jnp.exp(tot))
        state = decays[k] * state + bs
        total = total + tot
    ls_ref[0] = state
    grad = jnp.zeros((N, LANES), F32)
    for k in reversed(range(blocks)):
        grad = decays[k] * grad + bg_ref[0, k]
    lg_ref[0] = grad
    dec_ref[0] = jnp.broadcast_to(jnp.exp(total), (8, LANES))


def chain_kernel(
    size, ls_ref, lg_ref, dec_ref, sin_ref, gin_ref,
    fout, fin, bout, bin_, fsend, frecv, bsend, brecv,
):
    me = lax.axis_index("seq")
    chunks = ls_ref.shape[0]
    lag = 2
    barrier = pltpu.get_barrier_semaphore()

    @pl.when(me > 0)
    def _():
        pl.semaphore_signal(barrier, inc=1, device_id={"seq": me - 1}, device_id_type=MESH)

    @pl.when(me < size - 1)
    def _():
        pl.semaphore_signal(barrier, inc=1, device_id={"seq": me + 1}, device_id_type=MESH)

    pl.semaphore_wait(barrier, lax.min(me, 1) + lax.min(size - 1 - me, 1))

    def copy(out, into, send, recv, k, target):
        return pltpu.make_async_remote_copy(
            src_ref=out.at[k],
            dst_ref=into.at[k],
            send_sem=send.at[k],
            recv_sem=recv.at[k],
            device_id={"seq": target},
            device_id_type=MESH,
        )

    def forward(k):
        @pl.when(me == 0)
        def _():
            sin_ref[k] = jnp.zeros((N, LANES), F32)
            fout[k] = ls_ref[k]

        @pl.when(me > 0)
        def _():
            copy(fout, fin, fsend, frecv, k, me - 1).wait_recv()
            got = fin[k]
            sin_ref[k] = got
            fout[k] = dec_ref[k][0:1, :] * got + ls_ref[k]

        @pl.when(me < size - 1)
        def _():
            copy(fout, fin, fsend, frecv, k, me + 1).start()

    def backward(k):
        @pl.when(me == size - 1)
        def _():
            gin_ref[k] = jnp.zeros((N, LANES), F32)
            bout[k] = lg_ref[k]

        @pl.when(me < size - 1)
        def _():
            copy(bout, bin_, bsend, brecv, k, me + 1).wait_recv()
            got = bin_[k]
            gin_ref[k] = got
            bout[k] = dec_ref[k][0:1, :] * got + lg_ref[k]

        @pl.when(me > 0)
        def _():
            copy(bout, bin_, bsend, brecv, k, me - 1).start()

    late_f = lax.max(0, 2 * me - (size - 1)) * lag
    late_b = lax.max(0, (size - 1) - 2 * me) * lag

    def turn(step, carry):
        kf = step - late_f
        kb = step - late_b

        @pl.when(jnp.logical_and(kf >= 0, kf < chunks))
        def _():
            forward(kf)

        @pl.when(jnp.logical_and(kb >= 0, kb < chunks))
        def _():
            backward(kb)

        return carry

    lax.fori_loop(0, chunks + (size - 1) * lag, turn, 0)

    def drain(k, carry):
        @pl.when(me < size - 1)
        def _():
            copy(fout, fin, fsend, frecv, k, me + 1).wait_send()

        @pl.when(me > 0)
        def _():
            copy(bout, bin_, bsend, brecv, k, me - 1).wait_send()

        return carry

    lax.fori_loop(0, chunks, drain, 0)


def greet(axis, size, me):
    barrier = pltpu.get_barrier_semaphore()
    for d in range(1, size):
        pl.semaphore_signal(
            barrier, inc=1, device_id={axis: lax.rem(me + d, size)}, device_id_type=MESH
        )
    pl.semaphore_wait(barrier, size - 1)


def share_kernel(size, in_ref, out_ref, got, send, recv):
    me = lax.axis_index("seq")
    greet("seq", size, me)

    def copy(d, owner, target):
        return pltpu.make_async_remote_copy(
            src_ref=in_ref,
            dst_ref=got.at[owner],
            send_sem=send.at[d],
            recv_sem=recv.at[owner],
            device_id={"seq": target},
            device_id_type=MESH,
        )

    for d in range(1, size):
        copy(d, me, lax.rem(me + d, size)).start()
    got[me] = in_ref[...]
    for d in range(1, size):
        source = lax.rem(me + size - d, size)
        copy(d, source, source).wait_recv()
    total = got[0]
    for i in range(1, size):
        total = total + got[i]
    out_ref[...] = total
    for d in range(1, size):
        copy(d, me, lax.rem(me + d, size)).wait_send()


def head_sum_kernel(size, in_ref, out_ref, got, send1, recv1, send2, recv2):
    me = lax.axis_index("head")
    greet("head", size, me)
    rows = in_ref.shape[0] // size

    def block(i):
        return pl.ds(pl.multiple_of(i * rows, rows), rows)

    def scatter(d, owner, target):
        return pltpu.make_async_remote_copy(
            src_ref=in_ref.at[block(target)],
            dst_ref=got.at[owner],
            send_sem=send1.at[d],
            recv_sem=recv1.at[owner],
            device_id={"head": target},
            device_id_type=MESH,
        )

    def gather(d, owner, target):
        return pltpu.make_async_remote_copy(
            src_ref=out_ref.at[block(owner)],
            dst_ref=out_ref.at[block(owner)],
            send_sem=send2.at[d],
            recv_sem=recv2.at[owner],
            device_id={"head": target},
            device_id_type=MESH,
        )

    for d in range(1, size):
        scatter(d, me, lax.rem(me + d, size)).start()
    got[me] = in_ref[block(me), :]
    for d in range(1, size):
        source = lax.rem(me + size - d, size)
        scatter(d, source, source).wait_recv()
    total = got[0]
    for i in range(1, size):
        total = total + got[i]
    out_ref[block(me), :] = total
    for d in range(1, size):
        gather(d, me, lax.rem(me + d, size)).start()
    for d in range(1, size):
        source = lax.rem(me + size - d, size)
        gather(d, source, source).wait_recv()
    for d in range(1, size):
        target = lax.rem(me + d, size)
        scatter(d, me, target).wait_send()
        gather(d, me, target).wait_send()


def main_kernel(
    halo_ref, x_ref, gy_ref, taps_ref, skip_ref, s_ref, run_ref, runt_ref,
    b_ref, c_ref, sc_ref, bs_ref, bg_ref, sin_ref, gin_ref,
    out_ref, gx_ref, tail_ref, first_ref, tapg_ref, skipg_ref, dbc_ref, u_ref, v_ref, bnd_ref,
    xp, gp, zs, gs, bh, bl, ch, cl,
):
    p = pl.program_id(0)
    frames = x_ref.shape[0]
    blocks = frames // BLOCK
    square = (BLOCK, BLOCK)

    @pl.when(p == 0)
    def _():
        bh[...], bl[...] = split(b_ref[...])
        ch[...], cl[...] = split(c_ref[...])
        gs[...] = jnp.zeros_like(gs)
        dbc_ref[...] = jnp.zeros_like(dbc_ref)
        u_ref[...] = jnp.zeros_like(u_ref)
        v_ref[...] = jnp.zeros_like(v_ref)
        bnd_ref[...] = jnp.zeros_like(bnd_ref)

    pre = conv_x_pre(xp, halo_ref, x_ref, taps_ref)
    gate = 1.0 / (1.0 + jnp.exp(-pre))
    xa = pre * gate
    slope = gate * (1.0 + pre * (1.0 - gate))
    back = lax.rem(LANES - 2 * p, LANES)
    causal = row_ids(square) >= lane_ids(square)
    low = lane_ids(square) < P_SIZE
    heads = jnp.where(
        lane_ids(square) == 2 * p + row_ids(square) // P_SIZE, 1.0, 0.0
    ).astype(BF16)
    nothing = jnp.zeros(square, BF16)

    runs = []
    decays = []
    for k in range(blocks):
        rolled = pltpu.roll(run_ref[rows_of(k), :], back, 1)
        runs.append(rolled)
        wide = pair_columns(rolled[BLOCK - 8 : BLOCK, :])
        decays.append(jnp.exp(wide[7:8, :]))
    grads = [None] * blocks
    grad = gin_ref[0]
    for k in reversed(range(blocks)):
        grads[k] = grad
        grad = decays[k] * grad + bg_ref[0, k]

    state = sin_ref[0]
    for k in range(blocks):
        rows = rows_of(k)
        x = xa[rows, :]
        gyh = gy_ref[rows, :]
        gy = gyh.astype(F32)
        run = pair_columns(runs[k])
        step = pair_columns(pltpu.roll(s_ref[rows, :], back, 1))
        reach = jnp.exp(run)
        to_end = jnp.exp(run[BLOCK - 1 : BLOCK, :] - run)
        xs = x * step
        xsh, xsl = split(xs)
        stored = split(state)
        graded = split(grads[k])
        b2 = (bh[rows, :], bl[rows, :])
        c2 = (ch[rows, :], cl[rows, :])
        gy_heads = jnp.concatenate(
            [jnp.where(low, gyh, nothing), jnp.where(low, nothing, gyh)], axis=0
        )
        prod = mm(gy_heads, xsh, NT) + mm(gy_heads, xsl, NT)
        weights = []
        score_grad = gs[k]
        for half in range(2):
            gap = runs[k][:, half : half + 1] - runt_ref[k, pl.ds(2 * p + half, 1), :]
            decay = jnp.exp(jnp.where(causal, gap, -jnp.inf))
            weights.append(split(sc_ref[k] * decay))
            score_grad = score_grad + decay * prod[half * BLOCK : (half + 1) * BLOCK, :]
        gs[k] = score_grad
        wh = jnp.concatenate([weights[0][0], weights[1][0]], axis=1)
        wl = jnp.concatenate([weights[0][1], weights[1][1]], axis=1)
        xh2 = jnp.concatenate(
            [jnp.where(low, xsh, nothing), jnp.where(low, nothing, xsh)], axis=0
        )
        xl2 = jnp.concatenate(
            [jnp.where(low, xsl, nothing), jnp.where(low, nothing, xsl)], axis=0
        )
        y_scan = mm(wh, xh2) + (mm(wh, xl2) + mm(wl, xh2)) + reach * dot3(c2, stored)
        tall_h = jnp.concatenate([weights[0][0], weights[1][0]], axis=0)
        tall_l = jnp.concatenate([weights[0][1], weights[1][1]], axis=0)
        z = mm(tall_h, gy_heads, TN) + mm(tall_l, gy_heads, TN) + to_end * dot3(b2, graded)
        out_ref[rows, :] = (y_scan + skip_ref[0:1, :] * x).astype(BF16)
        zs[rows, :] = z * step + skip_ref[0:1, :] * gy
        u2 = split(gy * y_scan)
        v2 = split(x * z)
        u_ref[rows, :] += mm(u2[0], heads) + mm(u2[1], heads)
        v_ref[rows, :] += mm(v2[0], heads) + mm(v2[1], heads)
        dbc_ref[rows, :N] += dot3(split(xs * to_end), graded, NT)
        dbc_ref[rows, N:] += dot3(split(gy * reach), stored, NT)
        state = decays[k] * state + bs_ref[0, k]
        crossing = jnp.broadcast_to(jnp.sum(state * grads[k], axis=0, keepdims=True), (8, LANES))
        cross2 = split(crossing)
        bnd_ref[k] += mm(cross2[0], heads) + mm(cross2[1], heads)

    skipg_ref[...] = jnp.broadcast_to(
        jnp.sum(xa * gy_ref[...].astype(F32), axis=0, keepdims=True), (8, LANES)
    )
    g = zs[...] * slope
    gp[0:frames, :] = g
    gp[frames : frames + 8, :] = jnp.zeros((8, LANES), F32)
    gx = taps_ref[0:1, :] * gp[3 : 3 + frames, :]
    for k in range(1, 4):
        gx = gx + taps_ref[k : k + 1, :] * gp[3 - k : 3 - k + frames, :]
    gx_ref[...] = gx.astype(BF16)
    tail_ref[...] = gx[frames - 8 :, :]
    first_ref[...] = g[0:8, :]
    for k in range(4):
        tapg_ref[k : k + 1, :] = jnp.sum(
            g * xp[5 + k : 5 + k + frames, :], axis=0, keepdims=True
        )

    @pl.when(p == pl.num_programs(0) - 1)
    def _():
        for k in range(blocks):
            rows = rows_of(k)
            gk = split(gs[k])
            gt = split(gs[k].T)
            dbc_ref[rows, :N] += dot3(gt, (ch[rows, :], cl[rows, :]))
            dbc_ref[rows, N:] += dot3(gk, (bh[rows, :], bl[rows, :]))


def local(x_raw, bc_raw, dt_raw, conv_x, conv_bc, dt_bias, a_log, skip_d, d_out):
    margin = conv_x.shape[0] - 1
    frames, width = x_raw.shape
    head_count = dt_raw.shape[1]
    blocks = frames // BLOCK
    pairs = width // LANES
    size = lax.axis_size("seq")
    shape = jax.ShapeDtypeStruct

    tails = jnp.concatenate([x_raw[-margin:], bc_raw[-margin:]], axis=1)
    before = shifted(tails, "seq", 1)
    halo = jnp.pad(before.astype(F32), ((8 - margin, 0), (0, 0)))
    x_halo = halo[:, :width]
    bc_ext = jnp.concatenate([halo[:, width:], bc_raw.astype(F32)], axis=0)
    raw_sum = dt_raw + dt_bias
    step_size = jax.nn.softplus(raw_sum)
    rates = jnp.exp(a_log)
    log_decay = -step_size * rates
    padding = ((0, 0), (0, LANES - head_count))
    s_pad = jnp.pad(step_size, padding)
    la_pad = jnp.pad(log_decay, padding)
    skip_wide = jnp.broadcast_to(jnp.repeat(skip_d, P_SIZE)[None], (8, width))

    def whole(*dims):
        return pl.BlockSpec(dims, lambda p: (0,) * len(dims))

    def columns(rows):
        return pl.BlockSpec((rows, LANES), lambda p: (0, p))

    def pair(*dims):
        return pl.BlockSpec((1,) + dims, lambda p: (p,) + (0,) * len(dims))

    bs, bg, ls, lg, dec, run, b_act, c_act, scores, runt = pl.pallas_call(
        terms_kernel,
        grid=(pairs,),
        in_specs=[
            columns(8), columns(frames), columns(frames), columns(4),
            whole(frames + 8, 2 * N), whole(4, 2 * N), whole(frames, LANES), whole(frames, LANES),
        ],
        out_specs=[
            pair(blocks, N, LANES), pair(blocks, N, LANES), pair(N, LANES), pair(N, LANES),
            pair(8, LANES), whole(frames, LANES), whole(frames, N), whole(frames, N),
            whole(blocks, BLOCK, BLOCK), whole(blocks, LANES, BLOCK),
        ],
        out_shape=[
            shape((pairs, blocks, N, LANES), F32), shape((pairs, blocks, N, LANES), F32),
            shape((pairs, N, LANES), F32), shape((pairs, N, LANES), F32),
            shape((pairs, 8, LANES), F32), shape((frames, LANES), F32),
            shape((frames, N), F32), shape((frames, N), F32),
            shape((blocks, BLOCK, BLOCK), F32), shape((blocks, LANES, BLOCK), F32),
        ],
        scratch_shapes=[pltpu.VMEM((frames + 8, LANES), F32)]
        + [pltpu.VMEM((blocks, N, BLOCK), BF16)] * 4,
        compiler_params=pltpu.CompilerParams(vmem_limit_bytes=VMEM_LIMIT),
        name="terms",
    )(x_halo, x_raw, d_out, conv_x, bc_ext, conv_bc, s_pad, la_pad)

    in_vmem = pl.BlockSpec(memory_space=pltpu.VMEM)
    state_in, grad_in = pl.pallas_call(
        lambda *refs: chain_kernel(size, *refs),
        in_specs=[in_vmem] * 3,
        out_specs=[in_vmem] * 2,
        out_shape=[shape((pairs, N, LANES), F32)] * 2,
        scratch_shapes=[pltpu.VMEM((pairs, N, LANES), F32)] * 4
        + [pltpu.SemaphoreType.DMA((pairs,))] * 4,
        compiler_params=pltpu.CompilerParams(
            collective_id=0, has_side_effects=True, vmem_limit_bytes=VMEM_LIMIT
        ),
        name="chain",
    )(ls, lg, dec)

    layer_out, grad_x, tail, first, tap_grad, skip_grad, bc_local, u, v, bnd = pl.pallas_call(
        main_kernel,
        grid=(pairs,),
        in_specs=[
            columns(8), columns(frames), columns(frames), columns(4), columns(8),
            whole(frames, LANES), whole(frames, LANES), whole(blocks, LANES, BLOCK),
            whole(frames, N), whole(frames, N), whole(blocks, BLOCK, BLOCK),
            pair(blocks, N, LANES), pair(blocks, N, LANES), pair(N, LANES), pair(N, LANES),
        ],
        out_specs=[
            columns(frames), columns(frames), columns(8), columns(8), columns(4), columns(8),
            whole(frames, 2 * N), whole(frames, LANES), whole(frames, LANES),
            whole(blocks, 8, LANES),
        ],
        out_shape=[
            shape((frames, width), BF16), shape((frames, width), BF16),
            shape((8, width), F32), shape((8, width), F32), shape((4, width), F32),
            shape((8, width), F32), shape((frames, 2 * N), F32),
            shape((frames, LANES), F32), shape((frames, LANES), F32),
            shape((blocks, 8, LANES), F32),
        ],
        scratch_shapes=[
            pltpu.VMEM((frames + 8, LANES), F32), pltpu.VMEM((frames + 8, LANES), F32),
            pltpu.VMEM((frames, LANES), F32), pltpu.VMEM((blocks, BLOCK, BLOCK), F32),
        ]
        + [pltpu.VMEM((frames, N), BF16)] * 4,
        compiler_params=pltpu.CompilerParams(vmem_limit_bytes=VMEM_LIMIT),
        name="main",
    )(
        x_halo, x_raw, d_out, conv_x, skip_wide, s_pad, run, runt,
        b_act, c_act, scores, bs, bg, state_in, grad_in,
    )

    heads = lax.axis_size("head")
    bc_total = pl.pallas_call(
        lambda *refs: head_sum_kernel(heads, *refs),
        in_specs=[in_vmem],
        out_specs=in_vmem,
        out_shape=shape((frames, 2 * N), F32),
        scratch_shapes=[pltpu.VMEM((heads, frames // heads, 2 * N), F32)]
        + [pltpu.SemaphoreType.DMA((heads,))] * 4,
        compiler_params=pltpu.CompilerParams(
            collective_id=1, has_side_effects=True, vmem_limit_bytes=VMEM_LIMIT
        ),
        name="head_sum",
    )(bc_local)

    bc_pre = conv_bc[0] * bc_ext[5 : 5 + frames]
    for k in range(1, 4):
        bc_pre = bc_pre + conv_bc[k] * bc_ext[5 + k : 5 + k + frames]
    gate = jax.nn.sigmoid(bc_pre)
    bc_grad = bc_total * (gate * (1.0 + bc_pre * (1.0 - gate)))
    conv_bc_grad = jnp.stack(
        [jnp.sum(bc_grad * bc_ext[5 + k : 5 + k + frames], axis=0) for k in range(4)]
    )
    after = shifted(jnp.concatenate([first[:margin], bc_grad[:margin]], axis=1), "seq", -1)
    bc_spread = jnp.concatenate([bc_grad, after[:, width:]], axis=0)
    grad_bc = conv_bc[0] * bc_spread[3 : 3 + frames]
    for k in range(1, 4):
        grad_bc = grad_bc + conv_bc[k] * bc_spread[3 - k : 3 - k + frames]
    x_after = jnp.pad(after[:, :width], ((margin, 0), (0, 0)))
    patch = tail[8 - margin :]
    for k in range(margin):
        patch = patch + conv_x[k] * x_after[3 - k : 6 - k]
    grad_x = lax.dynamic_update_slice(grad_x, patch.astype(BF16), (frames - margin, 0))

    u = u[:, :head_count]
    v = v[:, :head_count]
    net = (u - step_size * v).reshape(blocks, BLOCK, head_count)
    upper = (jnp.arange(BLOCK)[:, None] <= jnp.arange(BLOCK)[None, :]).astype(F32)
    g_log = jnp.einsum("tq,kqh->kth", upper, net, precision=lax.Precision.HIGHEST)
    g_log = (g_log + bnd[:, 0:1, :head_count]).reshape(frames, head_count)
    grad_steps = (v - g_log * rates) * jax.nn.sigmoid(raw_sum)
    skip_part = jnp.sum(skip_grad[0].reshape(head_count, P_SIZE), axis=1)
    flat = jnp.concatenate(
        [
            tap_grad.reshape(-1),
            conv_bc_grad.reshape(-1),
            jnp.sum(grad_steps, axis=0),
            jnp.sum(g_log * log_decay, axis=0),
            skip_part,
        ]
    )
    lines = -(-flat.shape[0] // (8 * LANES)) * 8
    flat = jnp.pad(flat, (0, lines * LANES - flat.shape[0])).reshape(lines, LANES)
    summed = pl.pallas_call(
        lambda *refs: share_kernel(size, *refs),
        in_specs=[in_vmem],
        out_specs=in_vmem,
        out_shape=shape((lines, LANES), F32),
        scratch_shapes=[pltpu.VMEM((size, lines, LANES), F32)]
        + [pltpu.SemaphoreType.DMA((size,))] * 2,
        compiler_params=pltpu.CompilerParams(
            collective_id=2, has_side_effects=True, vmem_limit_bytes=VMEM_LIMIT
        ),
        name="share",
    )(flat).reshape(-1)
    cuts = [4 * width, 8 * N, head_count, head_count, head_count]
    parts = []
    at = 0
    for cut in cuts:
        parts.append(summed[at : at + cut])
        at += cut
    return (
        layer_out,
        grad_x,
        grad_bc,
        grad_steps,
        parts[0].reshape(4, width),
        parts[1].reshape(4, 2 * N),
        parts[2],
        parts[3],
        parts[4],
    )


def solution(mesh):
    placed = (
        P("seq", "head"),
        P("seq", None),
        P("seq", "head"),
        P(None, "head"),
        P(),
        P("head"),
        P("head"),
        P("head"),
        P("seq", "head"),
    )
    return jax.shard_map(
        local,
        mesh=mesh,
        in_specs=placed,
        out_specs=(
            P("seq", "head"),
            P("seq", "head"),
            P("seq", None),
            P("seq", "head"),
            P(None, "head"),
            P(),
            P("head"),
            P("head"),
            P("head"),
        ),
        check_vma=False,
    )
```

```python
import jax
import jax.numpy as jnp
from jax import lax
from jax.experimental import pallas as pl
from jax.experimental.pallas import tpu as pltpu
from jax.sharding import PartitionSpec as P

P_SIZE = 64
N = 128
BLOCK = 128
LANES = 128
F32 = jnp.float32
BF16 = jnp.bfloat16
NN = (((1,), (0,)), ((), ()))
NT = (((1,), (1,)), ((), ()))
TN = (((0,), (0,)), ((), ()))
MESH = pl.DeviceIdType.MESH
VMEM_LIMIT = 44 * 2**20


def shifted(block, axis, distance):
    devices = range(lax.axis_size(axis))
    route = [(i - distance, i) for i in devices if i - distance in devices]
    return lax.ppermute(block, axis, route)


def split(a):
    high = a.astype(BF16)
    return high, (a - high.astype(F32)).astype(BF16)


def mm(a, b, dims=NN):
    return lax.dot_general(a, b, dims, preferred_element_type=F32)


def dot3(a, b, dims=NN):
    return mm(a[0], b[0], dims) + (mm(a[0], b[1], dims) + mm(a[1], b[0], dims))


def exact(a, b, dims=NN):
    return lax.dot_general(
        a, b, dims, precision=lax.Precision.HIGHEST, preferred_element_type=F32
    )


def silu(pre):
    return pre / (1.0 + jnp.exp(-pre))


def lane_ids(shape):
    return lax.broadcasted_iota(jnp.int32, shape, 1)


def row_ids(shape):
    return lax.broadcasted_iota(jnp.int32, shape, 0)


def rows_of(k):
    return slice(k * BLOCK, (k + 1) * BLOCK)


def pair_columns(rolled):
    first = jnp.broadcast_to(rolled[:, 0:1], rolled.shape)
    second = jnp.broadcast_to(rolled[:, 1:2], rolled.shape)
    return jnp.where(lane_ids(rolled.shape) < P_SIZE, first, second)


def conv_x_pre(xp, halo_ref, x_ref, taps_ref):
    frames = x_ref.shape[0]
    xp[0:8, :] = halo_ref[...]
    xp[8 : 8 + frames, :] = x_ref[...].astype(F32)
    pre = taps_ref[0:1, :] * xp[5 : 5 + frames, :]
    for k in range(1, 4):
        pre = pre + taps_ref[k : k + 1, :] * xp[5 + k : 5 + k + frames, :]
    return pre


def terms_kernel(
    halo_ref, x_ref, gy_ref, taps_ref, bc_ref, taps_bc_ref, s_ref, la_ref,
    bs_ref, bg_ref, ls_ref, lg_ref, dec_ref, run_ref, b_ref, c_ref, sc_ref, runt_ref,
    xp, bth, btl, cth, ctl,
):
    p = pl.program_id(0)
    frames = x_ref.shape[0]
    blocks = frames // BLOCK

    @pl.when(p == 0)
    def _():
        square = (BLOCK, BLOCK)
        tril = jnp.where(row_ids(square) >= lane_ids(square), 1.0, 0.0).astype(F32)
        pre = taps_bc_ref[0:1, :] * bc_ref[5 : 5 + frames, :]
        for k in range(1, 4):
            pre = pre + taps_bc_ref[k : k + 1, :] * bc_ref[5 + k : 5 + k + frames, :]
        act = silu(pre)
        b_ref[...] = act[:, :N]
        c_ref[...] = act[:, N:]
        for k in range(blocks):
            run = exact(tril, la_ref[rows_of(k), :])
            run_ref[rows_of(k), :] = run
            runt_ref[k] = run.T
            b = b_ref[rows_of(k), :]
            c = c_ref[rows_of(k), :]
            bth[k], btl[k] = split(b.T)
            cth[k], ctl[k] = split(c.T)
            sc_ref[k] = exact(c, b, NT)

    xa = silu(conv_x_pre(xp, halo_ref, x_ref, taps_ref))
    back = lax.rem(LANES - 2 * p, LANES)
    state = jnp.zeros((N, LANES), F32)
    total = jnp.zeros((1, LANES), F32)
    decays = []
    for k in range(blocks):
        run = pair_columns(pltpu.roll(run_ref[rows_of(k), :], back, 1))
        step = pair_columns(pltpu.roll(s_ref[rows_of(k), :], back, 1))
        tot = run[BLOCK - 1 : BLOCK, :]
        scaled = xa[rows_of(k), :] * (step * jnp.exp(tot - run))
        bs = dot3((bth[k], btl[k]), split(scaled))
        bs_ref[0, k] = bs
        bg_ref[0, k] = dot3(
            (cth[k], ctl[k]), split(gy_ref[rows_of(k), :].astype(F32) * jnp.exp(run))
        )
        decays.append(jnp.exp(tot))
        state = decays[k] * state + bs
        total = total + tot
    ls_ref[0] = state
    grad = jnp.zeros((N, LANES), F32)
    for k in reversed(range(blocks)):
        grad = decays[k] * grad + bg_ref[0, k]
    lg_ref[0] = grad
    dec_ref[0] = jnp.broadcast_to(jnp.exp(total), (8, LANES))


def chain_kernel(
    size, ls_ref, lg_ref, dec_ref, sin_ref, gin_ref,
    fout, fin, bout, bin_, fsend, frecv, bsend, brecv,
):
    me = lax.axis_index("seq")
    chunks = ls_ref.shape[0]
    lag = 2
    barrier = pltpu.get_barrier_semaphore()

    @pl.when(me > 0)
    def _():
        pl.semaphore_signal(barrier, inc=1, device_id={"seq": me - 1}, device_id_type=MESH)

    @pl.when(me < size - 1)
    def _():
        pl.semaphore_signal(barrier, inc=1, device_id={"seq": me + 1}, device_id_type=MESH)

    pl.semaphore_wait(barrier, lax.min(me, 1) + lax.min(size - 1 - me, 1))

    def copy(out, into, send, recv, k, target):
        return pltpu.make_async_remote_copy(
            src_ref=out.at[k],
            dst_ref=into.at[k],
            send_sem=send.at[k],
            recv_sem=recv.at[k],
            device_id={"seq": target},
            device_id_type=MESH,
        )

    def forward(k):
        @pl.when(me == 0)
        def _():
            sin_ref[k] = jnp.zeros((N, LANES), F32)
            fout[k] = ls_ref[k]

        @pl.when(me > 0)
        def _():
            copy(fout, fin, fsend, frecv, k, me - 1).wait_recv()
            got = fin[k]
            sin_ref[k] = got
            fout[k] = dec_ref[k][0:1, :] * got + ls_ref[k]

        @pl.when(me < size - 1)
        def _():
            copy(fout, fin, fsend, frecv, k, me + 1).start()

    def backward(k):
        @pl.when(me == size - 1)
        def _():
            gin_ref[k] = jnp.zeros((N, LANES), F32)
            bout[k] = lg_ref[k]

        @pl.when(me < size - 1)
        def _():
            copy(bout, bin_, bsend, brecv, k, me + 1).wait_recv()
            got = bin_[k]
            gin_ref[k] = got
            bout[k] = dec_ref[k][0:1, :] * got + lg_ref[k]

        @pl.when(me > 0)
        def _():
            copy(bout, bin_, bsend, brecv, k, me - 1).start()

    late_f = lax.max(0, 2 * me - (size - 1)) * lag
    late_b = lax.max(0, (size - 1) - 2 * me) * lag

    def turn(step, carry):
        kf = step - late_f
        kb = step - late_b

        @pl.when(jnp.logical_and(kf >= 0, kf < chunks))
        def _():
            forward(kf)

        @pl.when(jnp.logical_and(kb >= 0, kb < chunks))
        def _():
            backward(kb)

        return carry

    lax.fori_loop(0, chunks + (size - 1) * lag, turn, 0)

    def drain(k, carry):
        @pl.when(me < size - 1)
        def _():
            copy(fout, fin, fsend, frecv, k, me + 1).wait_send()

        @pl.when(me > 0)
        def _():
            copy(bout, bin_, bsend, brecv, k, me - 1).wait_send()

        return carry

    lax.fori_loop(0, chunks, drain, 0)


def greet(axis, size, me):
    barrier = pltpu.get_barrier_semaphore()
    for d in range(1, size):
        pl.semaphore_signal(
            barrier, inc=1, device_id={axis: lax.rem(me + d, size)}, device_id_type=MESH
        )
    pl.semaphore_wait(barrier, size - 1)


def share_kernel(size, in_ref, out_ref, got, send, recv):
    me = lax.axis_index("seq")
    greet("seq", size, me)

    def copy(d, owner, target):
        return pltpu.make_async_remote_copy(
            src_ref=in_ref,
            dst_ref=got.at[owner],
            send_sem=send.at[d],
            recv_sem=recv.at[owner],
            device_id={"seq": target},
            device_id_type=MESH,
        )

    for d in range(1, size):
        copy(d, me, lax.rem(me + d, size)).start()
    got[me] = in_ref[...]
    for d in range(1, size):
        source = lax.rem(me + size - d, size)
        copy(d, source, source).wait_recv()
    total = got[0]
    for i in range(1, size):
        total = total + got[i]
    out_ref[...] = total
    for d in range(1, size):
        copy(d, me, lax.rem(me + d, size)).wait_send()


def head_sum_kernel(size, in_ref, out_ref, got, send1, recv1, send2, recv2):
    me = lax.axis_index("head")
    greet("head", size, me)
    rows = in_ref.shape[0] // size

    def block(i):
        return pl.ds(pl.multiple_of(i * rows, rows), rows)

    def scatter(d, owner, target):
        return pltpu.make_async_remote_copy(
            src_ref=in_ref.at[block(target)],
            dst_ref=got.at[owner],
            send_sem=send1.at[d],
            recv_sem=recv1.at[owner],
            device_id={"head": target},
            device_id_type=MESH,
        )

    def gather(d, owner, target):
        return pltpu.make_async_remote_copy(
            src_ref=out_ref.at[block(owner)],
            dst_ref=out_ref.at[block(owner)],
            send_sem=send2.at[d, owner],
            recv_sem=recv2.at[owner],
            device_id={"head": target},
            device_id_type=MESH,
        )

    for d in range(1, size):
        scatter(d, me, lax.rem(me + d, size)).start()
    got[me] = in_ref[block(me), :]
    for d in range(1, size):
        source = lax.rem(me + size - d, size)
        scatter(d, source, source).wait_recv()
    total = got[0]
    for i in range(1, size):
        total = total + got[i]
    out_ref[block(me), :] = total
    def relay(owner, way, start):
        copy = gather(way, owner, me + 1 if way == 0 else me - 1)

        @pl.when(me < size - 1 if way == 0 else me > 0)
        def _():
            copy.start() if start else copy.wait_send()

    relay(me, 0, True)
    relay(me, 1, True)
    for k in range(1, size):
        @pl.when(me - k >= 0)
        def _():
            gather(0, me - k, me).wait_recv()
            relay(me - k, 0, True)

        @pl.when(me + k < size)
        def _():
            gather(1, me + k, me).wait_recv()
            relay(me + k, 1, True)

    for d in range(1, size):
        scatter(d, me, lax.rem(me + d, size)).wait_send()
    relay(me, 0, False)
    relay(me, 1, False)
    for k in range(1, size):
        @pl.when(me - k >= 0)
        def _():
            relay(me - k, 0, False)

        @pl.when(me + k < size)
        def _():
            relay(me + k, 1, False)


def main_kernel(
    halo_ref, x_ref, gy_ref, taps_ref, skip_ref, s_ref, run_ref, runt_ref,
    b_ref, c_ref, sc_ref, bs_ref, bg_ref, sin_ref, gin_ref,
    out_ref, gx_ref, tail_ref, first_ref, tapg_ref, skipg_ref, dbc_ref, u_ref, v_ref, bnd_ref,
    xp, gp, zs, gs, bh, bl, ch, cl,
):
    p = pl.program_id(0)
    frames = x_ref.shape[0]
    blocks = frames // BLOCK
    square = (BLOCK, BLOCK)

    @pl.when(p == 0)
    def _():
        bh[...], bl[...] = split(b_ref[...])
        ch[...], cl[...] = split(c_ref[...])
        gs[...] = jnp.zeros_like(gs)
        dbc_ref[...] = jnp.zeros_like(dbc_ref)
        u_ref[...] = jnp.zeros_like(u_ref)
        v_ref[...] = jnp.zeros_like(v_ref)
        bnd_ref[...] = jnp.zeros_like(bnd_ref)

    pre = conv_x_pre(xp, halo_ref, x_ref, taps_ref)
    gate = 1.0 / (1.0 + jnp.exp(-pre))
    xa = pre * gate
    slope = gate * (1.0 + pre * (1.0 - gate))
    back = lax.rem(LANES - 2 * p, LANES)
    causal = row_ids(square) >= lane_ids(square)
    low = lane_ids(square) < P_SIZE
    heads = jnp.where(
        lane_ids(square) == 2 * p + row_ids(square) // P_SIZE, 1.0, 0.0
    ).astype(BF16)
    nothing = jnp.zeros(square, BF16)

    runs = []
    decays = []
    for k in range(blocks):
        rolled = pltpu.roll(run_ref[rows_of(k), :], back, 1)
        runs.append(rolled)
        wide = pair_columns(rolled[BLOCK - 8 : BLOCK, :])
        decays.append(jnp.exp(wide[7:8, :]))
    grads = [None] * blocks
    grad = gin_ref[0]
    for k in reversed(range(blocks)):
        grads[k] = grad
        grad = decays[k] * grad + bg_ref[0, k]

    state = sin_ref[0]
    for k in range(blocks):
        rows = rows_of(k)
        x = xa[rows, :]
        gyh = gy_ref[rows, :]
        gy = gyh.astype(F32)
        run = pair_columns(runs[k])
        step = pair_columns(pltpu.roll(s_ref[rows, :], back, 1))
        reach = jnp.exp(run)
        to_end = jnp.exp(run[BLOCK - 1 : BLOCK, :] - run)
        xs = x * step
        xsh, xsl = split(xs)
        stored = split(state)
        graded = split(grads[k])
        b2 = (bh[rows, :], bl[rows, :])
        c2 = (ch[rows, :], cl[rows, :])
        gy_heads = jnp.concatenate(
            [jnp.where(low, gyh, nothing), jnp.where(low, nothing, gyh)], axis=0
        )
        prod = mm(gy_heads, xsh, NT) + mm(gy_heads, xsl, NT)
        weights = []
        score_grad = gs[k]
        for half in range(2):
            gap = runs[k][:, half : half + 1] - runt_ref[k, pl.ds(2 * p + half, 1), :]
            decay = jnp.exp(jnp.where(causal, gap, -jnp.inf))
            weights.append(split(sc_ref[k] * decay))
            score_grad = score_grad + decay * prod[half * BLOCK : (half + 1) * BLOCK, :]
        gs[k] = score_grad
        wh = jnp.concatenate([weights[0][0], weights[1][0]], axis=1)
        wl = jnp.concatenate([weights[0][1], weights[1][1]], axis=1)
        xh2 = jnp.concatenate(
            [jnp.where(low, xsh, nothing), jnp.where(low, nothing, xsh)], axis=0
        )
        xl2 = jnp.concatenate(
            [jnp.where(low, xsl, nothing), jnp.where(low, nothing, xsl)], axis=0
        )
        y_scan = mm(wh, xh2) + (mm(wh, xl2) + mm(wl, xh2)) + reach * dot3(c2, stored)
        tall_h = jnp.concatenate([weights[0][0], weights[1][0]], axis=0)
        tall_l = jnp.concatenate([weights[0][1], weights[1][1]], axis=0)
        z = mm(tall_h, gy_heads, TN) + mm(tall_l, gy_heads, TN) + to_end * dot3(b2, graded)
        out_ref[rows, :] = (y_scan + skip_ref[0:1, :] * x).astype(BF16)
        zs[rows, :] = z * step + skip_ref[0:1, :] * gy
        u2 = split(gy * y_scan)
        v2 = split(x * z)
        u_ref[rows, :] += mm(u2[0], heads) + mm(u2[1], heads)
        v_ref[rows, :] += mm(v2[0], heads) + mm(v2[1], heads)
        dbc_ref[rows, :N] += dot3(split(xs * to_end), graded, NT)
        dbc_ref[rows, N:] += dot3(split(gy * reach), stored, NT)
        state = decays[k] * state + bs_ref[0, k]
        crossing = jnp.broadcast_to(jnp.sum(state * grads[k], axis=0, keepdims=True), (8, LANES))
        cross2 = split(crossing)
        bnd_ref[k] += mm(cross2[0], heads) + mm(cross2[1], heads)

    skipg_ref[...] = jnp.broadcast_to(
        jnp.sum(xa * gy_ref[...].astype(F32), axis=0, keepdims=True), (8, LANES)
    )
    g = zs[...] * slope
    gp[0:frames, :] = g
    gp[frames : frames + 8, :] = jnp.zeros((8, LANES), F32)
    gx = taps_ref[0:1, :] * gp[3 : 3 + frames, :]
    for k in range(1, 4):
        gx = gx + taps_ref[k : k + 1, :] * gp[3 - k : 3 - k + frames, :]
    gx_ref[...] = gx.astype(BF16)
    tail_ref[...] = gx[frames - 8 :, :]
    first_ref[...] = g[0:8, :]
    for k in range(4):
        tapg_ref[k : k + 1, :] = jnp.sum(
            g * xp[5 + k : 5 + k + frames, :], axis=0, keepdims=True
        )

    @pl.when(p == pl.num_programs(0) - 1)
    def _():
        for k in range(blocks):
            rows = rows_of(k)
            gk = split(gs[k])
            gt = split(gs[k].T)
            dbc_ref[rows, :N] += dot3(gt, (ch[rows, :], cl[rows, :]))
            dbc_ref[rows, N:] += dot3(gk, (bh[rows, :], bl[rows, :]))


def local(x_raw, bc_raw, dt_raw, conv_x, conv_bc, dt_bias, a_log, skip_d, d_out):
    margin = conv_x.shape[0] - 1
    frames, width = x_raw.shape
    head_count = dt_raw.shape[1]
    blocks = frames // BLOCK
    pairs = width // LANES
    size = lax.axis_size("seq")
    shape = jax.ShapeDtypeStruct

    tails = jnp.concatenate([x_raw[-margin:], bc_raw[-margin:]], axis=1)
    before = shifted(tails, "seq", 1)
    halo = jnp.pad(before.astype(F32), ((8 - margin, 0), (0, 0)))
    x_halo = halo[:, :width]
    bc_ext = jnp.concatenate([halo[:, width:], bc_raw.astype(F32)], axis=0)
    raw_sum = dt_raw + dt_bias
    step_size = jax.nn.softplus(raw_sum)
    rates = jnp.exp(a_log)
    log_decay = -step_size * rates
    padding = ((0, 0), (0, LANES - head_count))
    s_pad = jnp.pad(step_size, padding)
    la_pad = jnp.pad(log_decay, padding)
    skip_wide = jnp.broadcast_to(jnp.repeat(skip_d, P_SIZE)[None], (8, width))

    def whole(*dims):
        return pl.BlockSpec(dims, lambda p: (0,) * len(dims))

    def columns(rows):
        return pl.BlockSpec((rows, LANES), lambda p: (0, p))

    def pair(*dims):
        return pl.BlockSpec((1,) + dims, lambda p: (p,) + (0,) * len(dims))

    bs, bg, ls, lg, dec, run, b_act, c_act, scores, runt = pl.pallas_call(
        terms_kernel,
        grid=(pairs,),
        in_specs=[
            columns(8), columns(frames), columns(frames), columns(4),
            whole(frames + 8, 2 * N), whole(4, 2 * N), whole(frames, LANES), whole(frames, LANES),
        ],
        out_specs=[
            pair(blocks, N, LANES), pair(blocks, N, LANES), pair(N, LANES), pair(N, LANES),
            pair(8, LANES), whole(frames, LANES), whole(frames, N), whole(frames, N),
            whole(blocks, BLOCK, BLOCK), whole(blocks, LANES, BLOCK),
        ],
        out_shape=[
            shape((pairs, blocks, N, LANES), F32), shape((pairs, blocks, N, LANES), F32),
            shape((pairs, N, LANES), F32), shape((pairs, N, LANES), F32),
            shape((pairs, 8, LANES), F32), shape((frames, LANES), F32),
            shape((frames, N), F32), shape((frames, N), F32),
            shape((blocks, BLOCK, BLOCK), F32), shape((blocks, LANES, BLOCK), F32),
        ],
        scratch_shapes=[pltpu.VMEM((frames + 8, LANES), F32)]
        + [pltpu.VMEM((blocks, N, BLOCK), BF16)] * 4,
        compiler_params=pltpu.CompilerParams(vmem_limit_bytes=VMEM_LIMIT),
        name="terms",
    )(x_halo, x_raw, d_out, conv_x, bc_ext, conv_bc, s_pad, la_pad)

    in_vmem = pl.BlockSpec(memory_space=pltpu.VMEM)
    state_in, grad_in = pl.pallas_call(
        lambda *refs: chain_kernel(size, *refs),
        in_specs=[in_vmem] * 3,
        out_specs=[in_vmem] * 2,
        out_shape=[shape((pairs, N, LANES), F32)] * 2,
        scratch_shapes=[pltpu.VMEM((pairs, N, LANES), F32)] * 4
        + [pltpu.SemaphoreType.DMA((pairs,))] * 4,
        compiler_params=pltpu.CompilerParams(
            collective_id=0, has_side_effects=True, vmem_limit_bytes=VMEM_LIMIT
        ),
        name="chain",
    )(ls, lg, dec)

    layer_out, grad_x, tail, first, tap_grad, skip_grad, bc_local, u, v, bnd = pl.pallas_call(
        main_kernel,
        grid=(pairs,),
        in_specs=[
            columns(8), columns(frames), columns(frames), columns(4), columns(8),
            whole(frames, LANES), whole(frames, LANES), whole(blocks, LANES, BLOCK),
            whole(frames, N), whole(frames, N), whole(blocks, BLOCK, BLOCK),
            pair(blocks, N, LANES), pair(blocks, N, LANES), pair(N, LANES), pair(N, LANES),
        ],
        out_specs=[
            columns(frames), columns(frames), columns(8), columns(8), columns(4), columns(8),
            whole(frames, 2 * N), whole(frames, LANES), whole(frames, LANES),
            whole(blocks, 8, LANES),
        ],
        out_shape=[
            shape((frames, width), BF16), shape((frames, width), BF16),
            shape((8, width), F32), shape((8, width), F32), shape((4, width), F32),
            shape((8, width), F32), shape((frames, 2 * N), F32),
            shape((frames, LANES), F32), shape((frames, LANES), F32),
            shape((blocks, 8, LANES), F32),
        ],
        scratch_shapes=[
            pltpu.VMEM((frames + 8, LANES), F32), pltpu.VMEM((frames + 8, LANES), F32),
            pltpu.VMEM((frames, LANES), F32), pltpu.VMEM((blocks, BLOCK, BLOCK), F32),
        ]
        + [pltpu.VMEM((frames, N), BF16)] * 4,
        compiler_params=pltpu.CompilerParams(vmem_limit_bytes=VMEM_LIMIT),
        name="main",
    )(
        x_halo, x_raw, d_out, conv_x, skip_wide, s_pad, run, runt,
        b_act, c_act, scores, bs, bg, state_in, grad_in,
    )

    heads = lax.axis_size("head")
    bc_total = pl.pallas_call(
        lambda *refs: head_sum_kernel(heads, *refs),
        in_specs=[in_vmem],
        out_specs=in_vmem,
        out_shape=shape((frames, 2 * N), F32),
        scratch_shapes=[pltpu.VMEM((heads, frames // heads, 2 * N), F32)]
        + [pltpu.SemaphoreType.DMA((heads,))] * 2
        + [pltpu.SemaphoreType.DMA((2, heads)), pltpu.SemaphoreType.DMA((heads,))],
        compiler_params=pltpu.CompilerParams(
            collective_id=1, has_side_effects=True, vmem_limit_bytes=VMEM_LIMIT
        ),
        name="head_sum",
    )(bc_local)

    bc_pre = conv_bc[0] * bc_ext[5 : 5 + frames]
    for k in range(1, 4):
        bc_pre = bc_pre + conv_bc[k] * bc_ext[5 + k : 5 + k + frames]
    gate = jax.nn.sigmoid(bc_pre)
    bc_grad = bc_total * (gate * (1.0 + bc_pre * (1.0 - gate)))
    conv_bc_grad = jnp.stack(
        [jnp.sum(bc_grad * bc_ext[5 + k : 5 + k + frames], axis=0) for k in range(4)]
    )
    after = shifted(jnp.concatenate([first[:margin], bc_grad[:margin]], axis=1), "seq", -1)
    bc_spread = jnp.concatenate([bc_grad, after[:, width:]], axis=0)
    grad_bc = conv_bc[0] * bc_spread[3 : 3 + frames]
    for k in range(1, 4):
        grad_bc = grad_bc + conv_bc[k] * bc_spread[3 - k : 3 - k + frames]
    x_after = jnp.pad(after[:, :width], ((margin, 0), (0, 0)))
    patch = tail[8 - margin :]
    for k in range(margin):
        patch = patch + conv_x[k] * x_after[3 - k : 6 - k]
    grad_x = lax.dynamic_update_slice(grad_x, patch.astype(BF16), (frames - margin, 0))

    u = u[:, :head_count]
    v = v[:, :head_count]
    net = (u - step_size * v).reshape(blocks, BLOCK, head_count)
    upper = (jnp.arange(BLOCK)[:, None] <= jnp.arange(BLOCK)[None, :]).astype(F32)
    g_log = jnp.einsum("tq,kqh->kth", upper, net, precision=lax.Precision.HIGHEST)
    g_log = (g_log + bnd[:, 0:1, :head_count]).reshape(frames, head_count)
    grad_steps = (v - g_log * rates) * jax.nn.sigmoid(raw_sum)
    skip_part = jnp.sum(skip_grad[0].reshape(head_count, P_SIZE), axis=1)
    flat = jnp.concatenate(
        [
            tap_grad.reshape(-1),
            conv_bc_grad.reshape(-1),
            jnp.sum(grad_steps, axis=0),
            jnp.sum(g_log * log_decay, axis=0),
            skip_part,
        ]
    )
    lines = -(-flat.shape[0] // (8 * LANES)) * 8
    flat = jnp.pad(flat, (0, lines * LANES - flat.shape[0])).reshape(lines, LANES)
    summed = pl.pallas_call(
        lambda *refs: share_kernel(size, *refs),
        in_specs=[in_vmem],
        out_specs=in_vmem,
        out_shape=shape((lines, LANES), F32),
        scratch_shapes=[pltpu.VMEM((size, lines, LANES), F32)]
        + [pltpu.SemaphoreType.DMA((size,))] * 2,
        compiler_params=pltpu.CompilerParams(
            collective_id=2, has_side_effects=True, vmem_limit_bytes=VMEM_LIMIT
        ),
        name="share",
    )(flat).reshape(-1)
    cuts = [4 * width, 8 * N, head_count, head_count, head_count]
    parts = []
    at = 0
    for cut in cuts:
        parts.append(summed[at : at + cut])
        at += cut
    return (
        layer_out,
        grad_x,
        grad_bc,
        grad_steps,
        parts[0].reshape(4, width),
        parts[1].reshape(4, 2 * N),
        parts[2],
        parts[3],
        parts[4],
    )


def solution(mesh):
    placed = (
        P("seq", "head"),
        P("seq", None),
        P("seq", "head"),
        P(None, "head"),
        P(),
        P("head"),
        P("head"),
        P("head"),
        P("seq", "head"),
    )
    return jax.shard_map(
        local,
        mesh=mesh,
        in_specs=placed,
        out_specs=(
            P("seq", "head"),
            P("seq", "head"),
            P("seq", None),
            P("seq", "head"),
            P(None, "head"),
            P(),
            P("head"),
            P("head"),
            P("head"),
        ),
        check_vma=False,
    )
```

```python
import jax
import jax.numpy as jnp
from jax import lax
from jax.experimental import pallas as pl
from jax.experimental.pallas import tpu as pltpu
from jax.sharding import PartitionSpec as P

P_SIZE = 64
N = 128
BLOCK = 128
LANES = 128
F32 = jnp.float32
BF16 = jnp.bfloat16
NN = (((1,), (0,)), ((), ()))
NT = (((1,), (1,)), ((), ()))
TN = (((0,), (0,)), ((), ()))
MESH = pl.DeviceIdType.MESH
VMEM_LIMIT = 44 * 2**20


def shifted(block, axis, distance):
    devices = range(lax.axis_size(axis))
    route = [(i - distance, i) for i in devices if i - distance in devices]
    return lax.ppermute(block, axis, route)


def split(a):
    high = a.astype(BF16)
    return high, (a - high.astype(F32)).astype(BF16)


def mm(a, b, dims=NN):
    return lax.dot_general(a, b, dims, preferred_element_type=F32)


def dot3(a, b, dims=NN):
    return mm(a[0], b[0], dims) + (mm(a[0], b[1], dims) + mm(a[1], b[0], dims))


def exact(a, b, dims=NN):
    return lax.dot_general(
        a, b, dims, precision=lax.Precision.HIGHEST, preferred_element_type=F32
    )


def silu(pre):
    return pre / (1.0 + jnp.exp(-pre))


def lane_ids(shape):
    return lax.broadcasted_iota(jnp.int32, shape, 1)


def row_ids(shape):
    return lax.broadcasted_iota(jnp.int32, shape, 0)


def rows_of(k):
    return slice(k * BLOCK, (k + 1) * BLOCK)


def pair_columns(rolled):
    first = jnp.broadcast_to(rolled[:, 0:1], rolled.shape)
    second = jnp.broadcast_to(rolled[:, 1:2], rolled.shape)
    return jnp.where(lane_ids(rolled.shape) < P_SIZE, first, second)


def conv_x_pre(xp, halo_ref, x_ref, taps_ref):
    frames = x_ref.shape[0]
    xp[0:8, :] = halo_ref[...]
    xp[8 : 8 + frames, :] = x_ref[...].astype(F32)
    pre = taps_ref[0:1, :] * xp[5 : 5 + frames, :]
    for k in range(1, 4):
        pre = pre + taps_ref[k : k + 1, :] * xp[5 + k : 5 + k + frames, :]
    return pre


def terms_kernel(
    halo_ref, x_ref, gy_ref, taps_ref, bc_ref, taps_bc_ref, s_ref, la_ref,
    bs_ref, bg_ref, ls_ref, lg_ref, dec_ref, run_ref, b_ref, c_ref, sc_ref, runt_ref,
    xp, bth, btl, cth, ctl,
):
    p = pl.program_id(0)
    frames = x_ref.shape[0]
    blocks = frames // BLOCK

    @pl.when(p == 0)
    def _():
        square = (BLOCK, BLOCK)
        tril = jnp.where(row_ids(square) >= lane_ids(square), 1.0, 0.0).astype(F32)
        pre = taps_bc_ref[0:1, :] * bc_ref[5 : 5 + frames, :]
        for k in range(1, 4):
            pre = pre + taps_bc_ref[k : k + 1, :] * bc_ref[5 + k : 5 + k + frames, :]
        act = silu(pre)
        b_ref[...] = act[:, :N]
        c_ref[...] = act[:, N:]
        for k in range(blocks):
            run = exact(tril, la_ref[rows_of(k), :])
            run_ref[rows_of(k), :] = run
            runt_ref[k] = run.T
            b = b_ref[rows_of(k), :]
            c = c_ref[rows_of(k), :]
            bth[k], btl[k] = split(b.T)
            cth[k], ctl[k] = split(c.T)
            sc_ref[k] = exact(c, b, NT)

    xa = silu(conv_x_pre(xp, halo_ref, x_ref, taps_ref))
    back = lax.rem(LANES - 2 * p, LANES)
    state = jnp.zeros((N, LANES), F32)
    total = jnp.zeros((1, LANES), F32)
    decays = []
    for k in range(blocks):
        run = pair_columns(pltpu.roll(run_ref[rows_of(k), :], back, 1))
        step = pair_columns(pltpu.roll(s_ref[rows_of(k), :], back, 1))
        tot = run[BLOCK - 1 : BLOCK, :]
        scaled = xa[rows_of(k), :] * (step * jnp.exp(tot - run))
        bs = dot3((bth[k], btl[k]), split(scaled))
        bs_ref[0, k] = bs
        bg_ref[0, k] = dot3(
            (cth[k], ctl[k]), split(gy_ref[rows_of(k), :].astype(F32) * jnp.exp(run))
        )
        decays.append(jnp.exp(tot))
        state = decays[k] * state + bs
        total = total + tot
    ls_ref[0] = state
    grad = jnp.zeros((N, LANES), F32)
    for k in reversed(range(blocks)):
        grad = decays[k] * grad + bg_ref[0, k]
    lg_ref[0] = grad
    dec_ref[0] = jnp.broadcast_to(jnp.exp(total), (8, LANES))


def chain_kernel(
    size, ls_ref, lg_ref, dec_ref, sin_ref, gin_ref,
    fout, fin, bout, bin_, fsend, frecv, bsend, brecv,
):
    me = lax.axis_index("seq")
    chunks, rows, _ = ls_ref.shape
    cut = chunks // dec_ref.shape[0]
    lag = 4
    barrier = pltpu.get_barrier_semaphore()

    @pl.when(me > 0)
    def _():
        pl.semaphore_signal(barrier, inc=1, device_id={"seq": me - 1}, device_id_type=MESH)

    @pl.when(me < size - 1)
    def _():
        pl.semaphore_signal(barrier, inc=1, device_id={"seq": me + 1}, device_id_type=MESH)

    pl.semaphore_wait(barrier, lax.min(me, 1) + lax.min(size - 1 - me, 1))

    def copy(out, into, send, recv, k, target):
        return pltpu.make_async_remote_copy(
            src_ref=out.at[k],
            dst_ref=into.at[k],
            send_sem=send.at[k],
            recv_sem=recv.at[k],
            device_id={"seq": target},
            device_id_type=MESH,
        )

    def forward(k):
        @pl.when(me == 0)
        def _():
            sin_ref[k] = jnp.zeros((rows, LANES), F32)
            fout[k] = ls_ref[k]

        @pl.when(me > 0)
        def _():
            copy(fout, fin, fsend, frecv, k, me - 1).wait_recv()
            fout[k] = dec_ref[k // cut][0:1, :] * fin[k] + ls_ref[k]

        @pl.when(me < size - 1)
        def _():
            copy(fout, fin, fsend, frecv, k, me + 1).start()

        @pl.when(me > 0)
        def _():
            sin_ref[k] = fin[k]

    def backward(k):
        @pl.when(me == size - 1)
        def _():
            gin_ref[k] = jnp.zeros((rows, LANES), F32)
            bout[k] = lg_ref[k]

        @pl.when(me < size - 1)
        def _():
            copy(bout, bin_, bsend, brecv, k, me + 1).wait_recv()
            bout[k] = dec_ref[k // cut][0:1, :] * bin_[k] + lg_ref[k]

        @pl.when(me > 0)
        def _():
            copy(bout, bin_, bsend, brecv, k, me - 1).start()

        @pl.when(me < size - 1)
        def _():
            gin_ref[k] = bin_[k]

    late_f = lax.max(0, 2 * me - (size - 1)) * lag
    late_b = lax.max(0, (size - 1) - 2 * me) * lag

    def turn(step, carry):
        kf = step - late_f
        kb = step - late_b

        @pl.when(jnp.logical_and(kf >= 0, kf < chunks))
        def _():
            forward(kf)

        @pl.when(jnp.logical_and(kb >= 0, kb < chunks))
        def _():
            backward(kb)

        return carry

    lax.fori_loop(0, chunks + (size - 1) * lag, turn, 0)

    def drain(k, carry):
        @pl.when(me < size - 1)
        def _():
            copy(fout, fin, fsend, frecv, k, me + 1).wait_send()

        @pl.when(me > 0)
        def _():
            copy(bout, bin_, bsend, brecv, k, me - 1).wait_send()

        return carry

    lax.fori_loop(0, chunks, drain, 0)


def greet(axis, size, me):
    barrier = pltpu.get_barrier_semaphore()
    for d in range(1, size):
        pl.semaphore_signal(
            barrier, inc=1, device_id={axis: lax.rem(me + d, size)}, device_id_type=MESH
        )
    pl.semaphore_wait(barrier, size - 1)


def share_kernel(size, in_ref, out_ref, got, send, recv):
    me = lax.axis_index("seq")
    greet("seq", size, me)

    def copy(d, owner, target):
        return pltpu.make_async_remote_copy(
            src_ref=in_ref,
            dst_ref=got.at[owner],
            send_sem=send.at[d],
            recv_sem=recv.at[owner],
            device_id={"seq": target},
            device_id_type=MESH,
        )

    for d in range(1, size):
        copy(d, me, lax.rem(me + d, size)).start()
    got[me] = in_ref[...]
    for d in range(1, size):
        source = lax.rem(me + size - d, size)
        copy(d, source, source).wait_recv()
    total = got[0]
    for i in range(1, size):
        total = total + got[i]
    out_ref[...] = total
    for d in range(1, size):
        copy(d, me, lax.rem(me + d, size)).wait_send()


def head_sum_kernel(size, in_ref, out_ref, got, send1, recv1, send2, recv2):
    me = lax.axis_index("head")
    greet("head", size, me)
    rows = in_ref.shape[0] // size

    def block(i):
        return pl.ds(pl.multiple_of(i * rows, rows), rows)

    def scatter(d, owner, target):
        return pltpu.make_async_remote_copy(
            src_ref=in_ref.at[block(target)],
            dst_ref=got.at[owner],
            send_sem=send1.at[d],
            recv_sem=recv1.at[owner],
            device_id={"head": target},
            device_id_type=MESH,
        )

    def gather(d, owner, target):
        return pltpu.make_async_remote_copy(
            src_ref=out_ref.at[block(owner)],
            dst_ref=out_ref.at[block(owner)],
            send_sem=send2.at[d],
            recv_sem=recv2.at[owner],
            device_id={"head": target},
            device_id_type=MESH,
        )

    for d in range(1, size):
        scatter(d, me, lax.rem(me + d, size)).start()
    got[me] = in_ref[block(me), :]
    for d in range(1, size):
        source = lax.rem(me + size - d, size)
        scatter(d, source, source).wait_recv()
    total = got[0]
    for i in range(1, size):
        total = total + got[i]
    out_ref[block(me), :] = total
    for d in range(1, size):
        gather(d, me, lax.rem(me + d, size)).start()
    for d in range(1, size):
        source = lax.rem(me + size - d, size)
        gather(d, source, source).wait_recv()
    for d in range(1, size):
        target = lax.rem(me + d, size)
        scatter(d, me, target).wait_send()
        gather(d, me, target).wait_send()


def main_kernel(
    halo_ref, x_ref, gy_ref, taps_ref, skip_ref, s_ref, run_ref, runt_ref,
    b_ref, c_ref, sc_ref, bs_ref, bg_ref, sin_ref, gin_ref,
    out_ref, gx_ref, tail_ref, first_ref, tapg_ref, skipg_ref, dbc_ref, u_ref, v_ref, bnd_ref,
    xp, gp, zs, gs, bh, bl, ch, cl,
):
    p = pl.program_id(0)
    frames = x_ref.shape[0]
    blocks = frames // BLOCK
    square = (BLOCK, BLOCK)

    @pl.when(p == 0)
    def _():
        bh[...], bl[...] = split(b_ref[...])
        ch[...], cl[...] = split(c_ref[...])
        gs[...] = jnp.zeros_like(gs)
        dbc_ref[...] = jnp.zeros_like(dbc_ref)
        u_ref[...] = jnp.zeros_like(u_ref)
        v_ref[...] = jnp.zeros_like(v_ref)
        bnd_ref[...] = jnp.zeros_like(bnd_ref)

    pre = conv_x_pre(xp, halo_ref, x_ref, taps_ref)
    gate = 1.0 / (1.0 + jnp.exp(-pre))
    xa = pre * gate
    slope = gate * (1.0 + pre * (1.0 - gate))
    back = lax.rem(LANES - 2 * p, LANES)
    causal = row_ids(square) >= lane_ids(square)
    low = lane_ids(square) < P_SIZE
    heads = jnp.where(
        lane_ids(square) == 2 * p + row_ids(square) // P_SIZE, 1.0, 0.0
    ).astype(BF16)
    nothing = jnp.zeros(square, BF16)

    runs = []
    decays = []
    for k in range(blocks):
        rolled = pltpu.roll(run_ref[rows_of(k), :], back, 1)
        runs.append(rolled)
        wide = pair_columns(rolled[BLOCK - 8 : BLOCK, :])
        decays.append(jnp.exp(wide[7:8, :]))
    grads = [None] * blocks
    grad = gin_ref[0]
    for k in reversed(range(blocks)):
        grads[k] = grad
        grad = decays[k] * grad + bg_ref[0, k]

    state = sin_ref[0]
    for k in range(blocks):
        rows = rows_of(k)
        x = xa[rows, :]
        gyh = gy_ref[rows, :]
        gy = gyh.astype(F32)
        run = pair_columns(runs[k])
        step = pair_columns(pltpu.roll(s_ref[rows, :], back, 1))
        reach = jnp.exp(run)
        to_end = jnp.exp(run[BLOCK - 1 : BLOCK, :] - run)
        xs = x * step
        xsh, xsl = split(xs)
        stored = split(state)
        graded = split(grads[k])
        b2 = (bh[rows, :], bl[rows, :])
        c2 = (ch[rows, :], cl[rows, :])
        gy_heads = jnp.concatenate(
            [jnp.where(low, gyh, nothing), jnp.where(low, nothing, gyh)], axis=0
        )
        prod = mm(gy_heads, xsh, NT) + mm(gy_heads, xsl, NT)
        weights = []
        score_grad = gs[k]
        for half in range(2):
            gap = runs[k][:, half : half + 1] - runt_ref[k, pl.ds(2 * p + half, 1), :]
            decay = jnp.exp(jnp.where(causal, gap, -jnp.inf))
            weights.append(split(sc_ref[k] * decay))
            score_grad = score_grad + decay * prod[half * BLOCK : (half + 1) * BLOCK, :]
        gs[k] = score_grad
        wh = jnp.concatenate([weights[0][0], weights[1][0]], axis=1)
        wl = jnp.concatenate([weights[0][1], weights[1][1]], axis=1)
        xh2 = jnp.concatenate(
            [jnp.where(low, xsh, nothing), jnp.where(low, nothing, xsh)], axis=0
        )
        xl2 = jnp.concatenate(
            [jnp.where(low, xsl, nothing), jnp.where(low, nothing, xsl)], axis=0
        )
        y_scan = mm(wh, xh2) + (mm(wh, xl2) + mm(wl, xh2)) + reach * dot3(c2, stored)
        tall_h = jnp.concatenate([weights[0][0], weights[1][0]], axis=0)
        tall_l = jnp.concatenate([weights[0][1], weights[1][1]], axis=0)
        z = mm(tall_h, gy_heads, TN) + mm(tall_l, gy_heads, TN) + to_end * dot3(b2, graded)
        out_ref[rows, :] = (y_scan + skip_ref[0:1, :] * x).astype(BF16)
        zs[rows, :] = z * step + skip_ref[0:1, :] * gy
        u2 = split(gy * y_scan)
        v2 = split(x * z)
        u_ref[rows, :] += mm(u2[0], heads) + mm(u2[1], heads)
        v_ref[rows, :] += mm(v2[0], heads) + mm(v2[1], heads)
        dbc_ref[rows, :N] += dot3(split(xs * to_end), graded, NT)
        dbc_ref[rows, N:] += dot3(split(gy * reach), stored, NT)
        state = decays[k] * state + bs_ref[0, k]
        crossing = jnp.broadcast_to(jnp.sum(state * grads[k], axis=0, keepdims=True), (8, LANES))
        cross2 = split(crossing)
        bnd_ref[k] += mm(cross2[0], heads) + mm(cross2[1], heads)

    skipg_ref[...] = jnp.broadcast_to(
        jnp.sum(xa * gy_ref[...].astype(F32), axis=0, keepdims=True), (8, LANES)
    )
    g = zs[...] * slope
    gp[0:frames, :] = g
    gp[frames : frames + 8, :] = jnp.zeros((8, LANES), F32)
    gx = taps_ref[0:1, :] * gp[3 : 3 + frames, :]
    for k in range(1, 4):
        gx = gx + taps_ref[k : k + 1, :] * gp[3 - k : 3 - k + frames, :]
    gx_ref[...] = gx.astype(BF16)
    tail_ref[...] = gx[frames - 8 :, :]
    first_ref[...] = g[0:8, :]
    for k in range(4):
        tapg_ref[k : k + 1, :] = jnp.sum(
            g * xp[5 + k : 5 + k + frames, :], axis=0, keepdims=True
        )

    @pl.when(p == pl.num_programs(0) - 1)
    def _():
        for k in range(blocks):
            rows = rows_of(k)
            gk = split(gs[k])
            gt = split(gs[k].T)
            dbc_ref[rows, :N] += dot3(gt, (ch[rows, :], cl[rows, :]))
            dbc_ref[rows, N:] += dot3(gk, (bh[rows, :], bl[rows, :]))


def local(x_raw, bc_raw, dt_raw, conv_x, conv_bc, dt_bias, a_log, skip_d, d_out):
    margin = conv_x.shape[0] - 1
    frames, width = x_raw.shape
    head_count = dt_raw.shape[1]
    blocks = frames // BLOCK
    pairs = width // LANES
    size = lax.axis_size("seq")
    shape = jax.ShapeDtypeStruct

    tails = jnp.concatenate([x_raw[-margin:], bc_raw[-margin:]], axis=1)
    before = shifted(tails, "seq", 1)
    halo = jnp.pad(before.astype(F32), ((8 - margin, 0), (0, 0)))
    x_halo = halo[:, :width]
    bc_ext = jnp.concatenate([halo[:, width:], bc_raw.astype(F32)], axis=0)
    raw_sum = dt_raw + dt_bias
    step_size = jax.nn.softplus(raw_sum)
    rates = jnp.exp(a_log)
    log_decay = -step_size * rates
    padding = ((0, 0), (0, LANES - head_count))
    s_pad = jnp.pad(step_size, padding)
    la_pad = jnp.pad(log_decay, padding)
    skip_wide = jnp.broadcast_to(jnp.repeat(skip_d, P_SIZE)[None], (8, width))

    def whole(*dims):
        return pl.BlockSpec(dims, lambda p: (0,) * len(dims))

    def columns(rows):
        return pl.BlockSpec((rows, LANES), lambda p: (0, p))

    def pair(*dims):
        return pl.BlockSpec((1,) + dims, lambda p: (p,) + (0,) * len(dims))

    bs, bg, ls, lg, dec, run, b_act, c_act, scores, runt = pl.pallas_call(
        terms_kernel,
        grid=(pairs,),
        in_specs=[
            columns(8), columns(frames), columns(frames), columns(4),
            whole(frames + 8, 2 * N), whole(4, 2 * N), whole(frames, LANES), whole(frames, LANES),
        ],
        out_specs=[
            pair(blocks, N, LANES), pair(blocks, N, LANES), pair(N, LANES), pair(N, LANES),
            pair(8, LANES), whole(frames, LANES), whole(frames, N), whole(frames, N),
            whole(blocks, BLOCK, BLOCK), whole(blocks, LANES, BLOCK),
        ],
        out_shape=[
            shape((pairs, blocks, N, LANES), F32), shape((pairs, blocks, N, LANES), F32),
            shape((pairs, N, LANES), F32), shape((pairs, N, LANES), F32),
            shape((pairs, 8, LANES), F32), shape((frames, LANES), F32),
            shape((frames, N), F32), shape((frames, N), F32),
            shape((blocks, BLOCK, BLOCK), F32), shape((blocks, LANES, BLOCK), F32),
        ],
        scratch_shapes=[pltpu.VMEM((frames + 8, LANES), F32)]
        + [pltpu.VMEM((blocks, N, BLOCK), BF16)] * 4,
        compiler_params=pltpu.CompilerParams(vmem_limit_bytes=VMEM_LIMIT),
        name="terms",
    )(x_halo, x_raw, d_out, conv_x, bc_ext, conv_bc, s_pad, la_pad)

    in_vmem = pl.BlockSpec(memory_space=pltpu.VMEM)
    pieces = (pairs * 2, N // 2, LANES)
    state_in, grad_in = pl.pallas_call(
        lambda *refs: chain_kernel(size, *refs),
        in_specs=[in_vmem] * 3,
        out_specs=[in_vmem] * 2,
        out_shape=[shape(pieces, F32)] * 2,
        scratch_shapes=[pltpu.VMEM(pieces, F32)] * 4
        + [pltpu.SemaphoreType.DMA((pieces[0],))] * 4,
        compiler_params=pltpu.CompilerParams(
            collective_id=0, has_side_effects=True, vmem_limit_bytes=VMEM_LIMIT
        ),
        name="chain",
    )(ls.reshape(pieces), lg.reshape(pieces), dec)
    state_in = state_in.reshape(pairs, N, LANES)
    grad_in = grad_in.reshape(pairs, N, LANES)

    layer_out, grad_x, tail, first, tap_grad, skip_grad, bc_local, u, v, bnd = pl.pallas_call(
        main_kernel,
        grid=(pairs,),
        in_specs=[
            columns(8), columns(frames), columns(frames), columns(4), columns(8),
            whole(frames, LANES), whole(frames, LANES), whole(blocks, LANES, BLOCK),
            whole(frames, N), whole(frames, N), whole(blocks, BLOCK, BLOCK),
            pair(blocks, N, LANES), pair(blocks, N, LANES), pair(N, LANES), pair(N, LANES),
        ],
        out_specs=[
            columns(frames), columns(frames), columns(8), columns(8), columns(4), columns(8),
            whole(frames, 2 * N), whole(frames, LANES), whole(frames, LANES),
            whole(blocks, 8, LANES),
        ],
        out_shape=[
            shape((frames, width), BF16), shape((frames, width), BF16),
            shape((8, width), F32), shape((8, width), F32), shape((4, width), F32),
            shape((8, width), F32), shape((frames, 2 * N), F32),
            shape((frames, LANES), F32), shape((frames, LANES), F32),
            shape((blocks, 8, LANES), F32),
        ],
        scratch_shapes=[
            pltpu.VMEM((frames + 8, LANES), F32), pltpu.VMEM((frames + 8, LANES), F32),
            pltpu.VMEM((frames, LANES), F32), pltpu.VMEM((blocks, BLOCK, BLOCK), F32),
        ]
        + [pltpu.VMEM((frames, N), BF16)] * 4,
        compiler_params=pltpu.CompilerParams(vmem_limit_bytes=VMEM_LIMIT),
        name="main",
    )(
        x_halo, x_raw, d_out, conv_x, skip_wide, s_pad, run, runt,
        b_act, c_act, scores, bs, bg, state_in, grad_in,
    )

    heads = lax.axis_size("head")
    bc_total = pl.pallas_call(
        lambda *refs: head_sum_kernel(heads, *refs),
        in_specs=[in_vmem],
        out_specs=in_vmem,
        out_shape=shape((frames, 2 * N), F32),
        scratch_shapes=[pltpu.VMEM((heads, frames // heads, 2 * N), F32)]
        + [pltpu.SemaphoreType.DMA((heads,))] * 4,
        compiler_params=pltpu.CompilerParams(
            collective_id=1, has_side_effects=True, vmem_limit_bytes=VMEM_LIMIT
        ),
        name="head_sum",
    )(bc_local)

    bc_pre = conv_bc[0] * bc_ext[5 : 5 + frames]
    for k in range(1, 4):
        bc_pre = bc_pre + conv_bc[k] * bc_ext[5 + k : 5 + k + frames]
    gate = jax.nn.sigmoid(bc_pre)
    bc_grad = bc_total * (gate * (1.0 + bc_pre * (1.0 - gate)))
    conv_bc_grad = jnp.stack(
        [jnp.sum(bc_grad * bc_ext[5 + k : 5 + k + frames], axis=0) for k in range(4)]
    )
    after = shifted(jnp.concatenate([first[:margin], bc_grad[:margin]], axis=1), "seq", -1)
    bc_spread = jnp.concatenate([bc_grad, after[:, width:]], axis=0)
    grad_bc = conv_bc[0] * bc_spread[3 : 3 + frames]
    for k in range(1, 4):
        grad_bc = grad_bc + conv_bc[k] * bc_spread[3 - k : 3 - k + frames]
    x_after = jnp.pad(after[:, :width], ((margin, 0), (0, 0)))
    patch = tail[8 - margin :]
    for k in range(margin):
        patch = patch + conv_x[k] * x_after[3 - k : 6 - k]
    grad_x = lax.dynamic_update_slice(grad_x, patch.astype(BF16), (frames - margin, 0))

    u = u[:, :head_count]
    v = v[:, :head_count]
    net = (u - step_size * v).reshape(blocks, BLOCK, head_count)
    upper = (jnp.arange(BLOCK)[:, None] <= jnp.arange(BLOCK)[None, :]).astype(F32)
    g_log = jnp.einsum("tq,kqh->kth", upper, net, precision=lax.Precision.HIGHEST)
    g_log = (g_log + bnd[:, 0:1, :head_count]).reshape(frames, head_count)
    grad_steps = (v - g_log * rates) * jax.nn.sigmoid(raw_sum)
    skip_part = jnp.sum(skip_grad[0].reshape(head_count, P_SIZE), axis=1)
    flat = jnp.concatenate(
        [
            tap_grad.reshape(-1),
            conv_bc_grad.reshape(-1),
            jnp.sum(grad_steps, axis=0),
            jnp.sum(g_log * log_decay, axis=0),
            skip_part,
        ]
    )
    lines = -(-flat.shape[0] // (8 * LANES)) * 8
    flat = jnp.pad(flat, (0, lines * LANES - flat.shape[0])).reshape(lines, LANES)
    summed = pl.pallas_call(
        lambda *refs: share_kernel(size, *refs),
        in_specs=[in_vmem],
        out_specs=in_vmem,
        out_shape=shape((lines, LANES), F32),
        scratch_shapes=[pltpu.VMEM((size, lines, LANES), F32)]
        + [pltpu.SemaphoreType.DMA((size,))] * 2,
        compiler_params=pltpu.CompilerParams(
            collective_id=2, has_side_effects=True, vmem_limit_bytes=VMEM_LIMIT
        ),
        name="share",
    )(flat).reshape(-1)
    cuts = [4 * width, 8 * N, head_count, head_count, head_count]
    parts = []
    at = 0
    for cut in cuts:
        parts.append(summed[at : at + cut])
        at += cut
    return (
        layer_out,
        grad_x,
        grad_bc,
        grad_steps,
        parts[0].reshape(4, width),
        parts[1].reshape(4, 2 * N),
        parts[2],
        parts[3],
        parts[4],
    )


def solution(mesh):
    placed = (
        P("seq", "head"),
        P("seq", None),
        P("seq", "head"),
        P(None, "head"),
        P(),
        P("head"),
        P("head"),
        P("head"),
        P("seq", "head"),
    )
    return jax.shard_map(
        local,
        mesh=mesh,
        in_specs=placed,
        out_specs=(
            P("seq", "head"),
            P("seq", "head"),
            P("seq", None),
            P("seq", "head"),
            P(None, "head"),
            P(),
            P("head"),
            P("head"),
            P("head"),
        ),
        check_vma=False,
    )
```

```python
import jax
import jax.numpy as jnp
from jax import lax
from jax.experimental import pallas as pl
from jax.experimental.pallas import tpu as pltpu
from jax.sharding import PartitionSpec as P

P_SIZE = 64
N = 128
BLOCK = 128
LANES = 128
F32 = jnp.float32
BF16 = jnp.bfloat16
NN = (((1,), (0,)), ((), ()))
NT = (((1,), (1,)), ((), ()))
TN = (((0,), (0,)), ((), ()))
MESH = pl.DeviceIdType.MESH
VMEM_LIMIT = 44 * 2**20


def shifted(block, axis, distance):
    devices = range(lax.axis_size(axis))
    route = [(i - distance, i) for i in devices if i - distance in devices]
    return lax.ppermute(block, axis, route)


def split(a):
    high = a.astype(BF16)
    return high, (a - high.astype(F32)).astype(BF16)


def mm(a, b, dims=NN):
    return lax.dot_general(a, b, dims, preferred_element_type=F32)


def dot3(a, b, dims=NN):
    return mm(a[0], b[0], dims) + (mm(a[0], b[1], dims) + mm(a[1], b[0], dims))


def exact(a, b, dims=NN):
    return lax.dot_general(
        a, b, dims, precision=lax.Precision.HIGHEST, preferred_element_type=F32
    )


def silu(pre):
    return pre / (1.0 + jnp.exp(-pre))


def lane_ids(shape):
    return lax.broadcasted_iota(jnp.int32, shape, 1)


def row_ids(shape):
    return lax.broadcasted_iota(jnp.int32, shape, 0)


def rows_of(k):
    return slice(k * BLOCK, (k + 1) * BLOCK)


def pair_columns(rolled):
    first = jnp.broadcast_to(rolled[:, 0:1], rolled.shape)
    second = jnp.broadcast_to(rolled[:, 1:2], rolled.shape)
    return jnp.where(lane_ids(rolled.shape) < P_SIZE, first, second)


def conv_x_pre(xp, halo_ref, x_ref, taps_ref):
    frames = x_ref.shape[0]
    xp[0:8, :] = halo_ref[...]
    xp[8 : 8 + frames, :] = x_ref[...].astype(F32)
    pre = taps_ref[0:1, :] * xp[5 : 5 + frames, :]
    for k in range(1, 4):
        pre = pre + taps_ref[k : k + 1, :] * xp[5 + k : 5 + k + frames, :]
    return pre


def terms_kernel(
    halo_ref, x_ref, gy_ref, taps_ref, bc_ref, taps_bc_ref, s_ref, la_ref,
    bs_ref, bg_ref, ls_ref, lg_ref, dec_ref, run_ref, b_ref, c_ref, sc_ref, runt_ref,
    xp, bth, btl, cth, ctl,
):
    p = pl.program_id(0)
    frames = x_ref.shape[0]
    blocks = frames // BLOCK

    @pl.when(p == 0)
    def _():
        square = (BLOCK, BLOCK)
        tril = jnp.where(row_ids(square) >= lane_ids(square), 1.0, 0.0).astype(F32)
        pre = taps_bc_ref[0:1, :] * bc_ref[5 : 5 + frames, :]
        for k in range(1, 4):
            pre = pre + taps_bc_ref[k : k + 1, :] * bc_ref[5 + k : 5 + k + frames, :]
        act = silu(pre)
        b_ref[...] = act[:, :N]
        c_ref[...] = act[:, N:]
        for k in range(blocks):
            run = exact(tril, la_ref[rows_of(k), :])
            run_ref[rows_of(k), :] = run
            runt_ref[k] = run.T
            b = b_ref[rows_of(k), :]
            c = c_ref[rows_of(k), :]
            bth[k], btl[k] = split(b.T)
            cth[k], ctl[k] = split(c.T)
            sc_ref[k] = exact(c, b, NT)

    xa = silu(conv_x_pre(xp, halo_ref, x_ref, taps_ref))
    back = lax.rem(LANES - 2 * p, LANES)
    state = jnp.zeros((N, LANES), F32)
    total = jnp.zeros((1, LANES), F32)
    decays = []
    for k in range(blocks):
        run = pair_columns(pltpu.roll(run_ref[rows_of(k), :], back, 1))
        step = pair_columns(pltpu.roll(s_ref[rows_of(k), :], back, 1))
        tot = run[BLOCK - 1 : BLOCK, :]
        scaled = xa[rows_of(k), :] * (step * jnp.exp(tot - run))
        bs = dot3((bth[k], btl[k]), split(scaled))
        bs_ref[0, k] = bs
        bg_ref[0, k] = dot3(
            (cth[k], ctl[k]), split(gy_ref[rows_of(k), :].astype(F32) * jnp.exp(run))
        )
        decays.append(jnp.exp(tot))
        state = decays[k] * state + bs
        total = total + tot
    ls_ref[0] = state
    grad = jnp.zeros((N, LANES), F32)
    for k in reversed(range(blocks)):
        grad = decays[k] * grad + bg_ref[0, k]
    lg_ref[0] = grad
    dec_ref[0] = jnp.broadcast_to(jnp.exp(total), (8, LANES))


def chain_kernel(
    size, ls_ref, lg_ref, dec_ref, sin_ref, gin_ref,
    fout, fin, bout, bin_, fsend, frecv, bsend, brecv,
):
    me = lax.axis_index("seq")
    chunks, rows, _ = ls_ref.shape
    cut = chunks // dec_ref.shape[0]
    lag = 4
    barrier = pltpu.get_barrier_semaphore()

    @pl.when(me > 0)
    def _():
        pl.semaphore_signal(barrier, inc=1, device_id={"seq": me - 1}, device_id_type=MESH)

    @pl.when(me < size - 1)
    def _():
        pl.semaphore_signal(barrier, inc=1, device_id={"seq": me + 1}, device_id_type=MESH)

    pl.semaphore_wait(barrier, lax.min(me, 1) + lax.min(size - 1 - me, 1))

    def copy(out, into, send, recv, k, target):
        return pltpu.make_async_remote_copy(
            src_ref=out.at[k],
            dst_ref=into.at[k],
            send_sem=send.at[k],
            recv_sem=recv.at[k],
            device_id={"seq": target},
            device_id_type=MESH,
        )

    def forward(k):
        @pl.when(me == 0)
        def _():
            sin_ref[k] = jnp.zeros((rows, LANES), F32)
            fout[k] = ls_ref[k]

        @pl.when(me > 0)
        def _():
            copy(fout, fin, fsend, frecv, k, me - 1).wait_recv()
            fout[k] = dec_ref[k // cut][0:1, :] * fin[k] + ls_ref[k]

        @pl.when(me < size - 1)
        def _():
            copy(fout, fin, fsend, frecv, k, me + 1).start()

        @pl.when(me > 0)
        def _():
            sin_ref[k] = fin[k]

    def backward(k):
        @pl.when(me == size - 1)
        def _():
            gin_ref[k] = jnp.zeros((rows, LANES), F32)
            bout[k] = lg_ref[k]

        @pl.when(me < size - 1)
        def _():
            copy(bout, bin_, bsend, brecv, k, me + 1).wait_recv()
            bout[k] = dec_ref[k // cut][0:1, :] * bin_[k] + lg_ref[k]

        @pl.when(me > 0)
        def _():
            copy(bout, bin_, bsend, brecv, k, me - 1).start()

        @pl.when(me < size - 1)
        def _():
            gin_ref[k] = bin_[k]

    late_f = lax.max(0, 2 * me - (size - 1)) * lag
    late_b = lax.max(0, (size - 1) - 2 * me) * lag

    def turn(step, carry):
        kf = step - late_f
        kb = step - late_b

        @pl.when(jnp.logical_and(kf >= 0, kf < chunks))
        def _():
            forward(kf)

        @pl.when(jnp.logical_and(kb >= 0, kb < chunks))
        def _():
            backward(kb)

        return carry

    lax.fori_loop(0, chunks + (size - 1) * lag, turn, 0)

    def drain(k, carry):
        @pl.when(me < size - 1)
        def _():
            copy(fout, fin, fsend, frecv, k, me + 1).wait_send()

        @pl.when(me > 0)
        def _():
            copy(bout, bin_, bsend, brecv, k, me - 1).wait_send()

        return carry

    lax.fori_loop(0, chunks, drain, 0)


def greet(axis, size, me):
    barrier = pltpu.get_barrier_semaphore()
    for d in range(1, size):
        pl.semaphore_signal(
            barrier, inc=1, device_id={axis: lax.rem(me + d, size)}, device_id_type=MESH
        )
    pl.semaphore_wait(barrier, size - 1)


def share_kernel(size, in_ref, out_ref, got, send, recv):
    me = lax.axis_index("seq")
    greet("seq", size, me)

    def copy(d, owner, target):
        return pltpu.make_async_remote_copy(
            src_ref=in_ref,
            dst_ref=got.at[owner],
            send_sem=send.at[d],
            recv_sem=recv.at[owner],
            device_id={"seq": target},
            device_id_type=MESH,
        )

    for d in range(1, size):
        copy(d, me, lax.rem(me + d, size)).start()
    got[me] = in_ref[...]
    for d in range(1, size):
        source = lax.rem(me + size - d, size)
        copy(d, source, source).wait_recv()
    total = got[0]
    for i in range(1, size):
        total = total + got[i]
    out_ref[...] = total
    for d in range(1, size):
        copy(d, me, lax.rem(me + d, size)).wait_send()


def head_sum_kernel(size, in_ref, out_ref, got, send1, recv1, send2, recv2):
    me = lax.axis_index("head")
    greet("head", size, me)
    rows = in_ref.shape[0] // size
    parts = 2
    part = rows // parts

    def block(i, h):
        return pl.ds(pl.multiple_of(i * rows + h * part, part), part)

    def scatter(d, h, owner, target):
        return pltpu.make_async_remote_copy(
            src_ref=in_ref.at[block(target, h)],
            dst_ref=got.at[owner, pl.ds(h * part, part)],
            send_sem=send1.at[h, d],
            recv_sem=recv1.at[h, owner],
            device_id={"head": target},
            device_id_type=MESH,
        )

    def gather(d, h, owner, target):
        return pltpu.make_async_remote_copy(
            src_ref=out_ref.at[block(owner, h)],
            dst_ref=out_ref.at[block(owner, h)],
            send_sem=send2.at[h, d],
            recv_sem=recv2.at[h, owner],
            device_id={"head": target},
            device_id_type=MESH,
        )

    for h in range(parts):
        for d in range(1, size):
            scatter(d, h, me, lax.rem(me + d, size)).start()
    for h in range(parts):
        got[me, h * part : (h + 1) * part] = in_ref[block(me, h), :]
        for d in range(1, size):
            source = lax.rem(me + size - d, size)
            scatter(d, h, source, source).wait_recv()
        total = got[0, h * part : (h + 1) * part]
        for i in range(1, size):
            total = total + got[i, h * part : (h + 1) * part]
        out_ref[block(me, h), :] = total
        for d in range(1, size):
            gather(d, h, me, lax.rem(me + d, size)).start()
    for h in range(parts):
        for d in range(1, size):
            source = lax.rem(me + size - d, size)
            gather(d, h, source, source).wait_recv()
        for d in range(1, size):
            target = lax.rem(me + d, size)
            scatter(d, h, me, target).wait_send()
            gather(d, h, me, target).wait_send()


def main_kernel(
    halo_ref, x_ref, gy_ref, taps_ref, skip_ref, s_ref, run_ref, runt_ref,
    b_ref, c_ref, sc_ref, bs_ref, bg_ref, sin_ref, gin_ref,
    out_ref, gx_ref, tail_ref, first_ref, tapg_ref, skipg_ref, dbc_ref, u_ref, v_ref, bnd_ref,
    xp, gp, zs, gs, bh, bl, ch, cl,
):
    p = pl.program_id(0)
    frames = x_ref.shape[0]
    blocks = frames // BLOCK
    square = (BLOCK, BLOCK)

    @pl.when(p == 0)
    def _():
        bh[...], bl[...] = split(b_ref[...])
        ch[...], cl[...] = split(c_ref[...])
        gs[...] = jnp.zeros_like(gs)
        dbc_ref[...] = jnp.zeros_like(dbc_ref)
        u_ref[...] = jnp.zeros_like(u_ref)
        v_ref[...] = jnp.zeros_like(v_ref)
        bnd_ref[...] = jnp.zeros_like(bnd_ref)

    pre = conv_x_pre(xp, halo_ref, x_ref, taps_ref)
    gate = 1.0 / (1.0 + jnp.exp(-pre))
    xa = pre * gate
    slope = gate * (1.0 + pre * (1.0 - gate))
    back = lax.rem(LANES - 2 * p, LANES)
    causal = row_ids(square) >= lane_ids(square)
    low = lane_ids(square) < P_SIZE
    heads = jnp.where(
        lane_ids(square) == 2 * p + row_ids(square) // P_SIZE, 1.0, 0.0
    ).astype(BF16)
    nothing = jnp.zeros(square, BF16)

    runs = []
    decays = []
    for k in range(blocks):
        rolled = pltpu.roll(run_ref[rows_of(k), :], back, 1)
        runs.append(rolled)
        wide = pair_columns(rolled[BLOCK - 8 : BLOCK, :])
        decays.append(jnp.exp(wide[7:8, :]))
    grads = [None] * blocks
    grad = gin_ref[0]
    for k in reversed(range(blocks)):
        grads[k] = grad
        grad = decays[k] * grad + bg_ref[0, k]

    state = sin_ref[0]
    for k in range(blocks):
        rows = rows_of(k)
        x = xa[rows, :]
        gyh = gy_ref[rows, :]
        gy = gyh.astype(F32)
        run = pair_columns(runs[k])
        step = pair_columns(pltpu.roll(s_ref[rows, :], back, 1))
        reach = jnp.exp(run)
        to_end = jnp.exp(run[BLOCK - 1 : BLOCK, :] - run)
        xs = x * step
        xsh, xsl = split(xs)
        stored = split(state)
        graded = split(grads[k])
        b2 = (bh[rows, :], bl[rows, :])
        c2 = (ch[rows, :], cl[rows, :])
        gy_heads = jnp.concatenate(
            [jnp.where(low, gyh, nothing), jnp.where(low, nothing, gyh)], axis=0
        )
        prod = mm(gy_heads, xsh, NT) + mm(gy_heads, xsl, NT)
        weights = []
        score_grad = gs[k]
        for half in range(2):
            gap = runs[k][:, half : half + 1] - runt_ref[k, pl.ds(2 * p + half, 1), :]
            decay = jnp.exp(jnp.where(causal, gap, -jnp.inf))
            weights.append(split(sc_ref[k] * decay))
            score_grad = score_grad + decay * prod[half * BLOCK : (half + 1) * BLOCK, :]
        gs[k] = score_grad
        wh = jnp.concatenate([weights[0][0], weights[1][0]], axis=1)
        wl = jnp.concatenate([weights[0][1], weights[1][1]], axis=1)
        xh2 = jnp.concatenate(
            [jnp.where(low, xsh, nothing), jnp.where(low, nothing, xsh)], axis=0
        )
        xl2 = jnp.concatenate(
            [jnp.where(low, xsl, nothing), jnp.where(low, nothing, xsl)], axis=0
        )
        y_scan = mm(wh, xh2) + (mm(wh, xl2) + mm(wl, xh2)) + reach * dot3(c2, stored)
        tall_h = jnp.concatenate([weights[0][0], weights[1][0]], axis=0)
        tall_l = jnp.concatenate([weights[0][1], weights[1][1]], axis=0)
        z = mm(tall_h, gy_heads, TN) + mm(tall_l, gy_heads, TN) + to_end * dot3(b2, graded)
        out_ref[rows, :] = (y_scan + skip_ref[0:1, :] * x).astype(BF16)
        zs[rows, :] = z * step + skip_ref[0:1, :] * gy
        u2 = split(gy * y_scan)
        v2 = split(x * z)
        u_ref[rows, :] += mm(u2[0], heads) + mm(u2[1], heads)
        v_ref[rows, :] += mm(v2[0], heads) + mm(v2[1], heads)
        dbc_ref[rows, :N] += dot3(split(xs * to_end), graded, NT)
        dbc_ref[rows, N:] += dot3(split(gy * reach), stored, NT)
        state = decays[k] * state + bs_ref[0, k]
        crossing = jnp.broadcast_to(jnp.sum(state * grads[k], axis=0, keepdims=True), (8, LANES))
        cross2 = split(crossing)
        bnd_ref[k] += mm(cross2[0], heads) + mm(cross2[1], heads)

    skipg_ref[...] = jnp.broadcast_to(
        jnp.sum(xa * gy_ref[...].astype(F32), axis=0, keepdims=True), (8, LANES)
    )
    g = zs[...] * slope
    gp[0:frames, :] = g
    gp[frames : frames + 8, :] = jnp.zeros((8, LANES), F32)
    gx = taps_ref[0:1, :] * gp[3 : 3 + frames, :]
    for k in range(1, 4):
        gx = gx + taps_ref[k : k + 1, :] * gp[3 - k : 3 - k + frames, :]
    gx_ref[...] = gx.astype(BF16)
    tail_ref[...] = gx[frames - 8 :, :]
    first_ref[...] = g[0:8, :]
    for k in range(4):
        tapg_ref[k : k + 1, :] = jnp.sum(
            g * xp[5 + k : 5 + k + frames, :], axis=0, keepdims=True
        )

    @pl.when(p == pl.num_programs(0) - 1)
    def _():
        for k in range(blocks):
            rows = rows_of(k)
            gk = split(gs[k])
            gt = split(gs[k].T)
            dbc_ref[rows, :N] += dot3(gt, (ch[rows, :], cl[rows, :]))
            dbc_ref[rows, N:] += dot3(gk, (bh[rows, :], bl[rows, :]))


def local(x_raw, bc_raw, dt_raw, conv_x, conv_bc, dt_bias, a_log, skip_d, d_out):
    margin = conv_x.shape[0] - 1
    frames, width = x_raw.shape
    head_count = dt_raw.shape[1]
    blocks = frames // BLOCK
    pairs = width // LANES
    size = lax.axis_size("seq")
    shape = jax.ShapeDtypeStruct

    tails = jnp.concatenate([x_raw[-margin:], bc_raw[-margin:]], axis=1)
    before = shifted(tails, "seq", 1)
    halo = jnp.pad(before.astype(F32), ((8 - margin, 0), (0, 0)))
    x_halo = halo[:, :width]
    bc_ext = jnp.concatenate([halo[:, width:], bc_raw.astype(F32)], axis=0)
    raw_sum = dt_raw + dt_bias
    step_size = jax.nn.softplus(raw_sum)
    rates = jnp.exp(a_log)
    log_decay = -step_size * rates
    padding = ((0, 0), (0, LANES - head_count))
    s_pad = jnp.pad(step_size, padding)
    la_pad = jnp.pad(log_decay, padding)
    skip_wide = jnp.broadcast_to(jnp.repeat(skip_d, P_SIZE)[None], (8, width))

    def whole(*dims):
        return pl.BlockSpec(dims, lambda p: (0,) * len(dims))

    def columns(rows):
        return pl.BlockSpec((rows, LANES), lambda p: (0, p))

    def pair(*dims):
        return pl.BlockSpec((1,) + dims, lambda p: (p,) + (0,) * len(dims))

    bs, bg, ls, lg, dec, run, b_act, c_act, scores, runt = pl.pallas_call(
        terms_kernel,
        grid=(pairs,),
        in_specs=[
            columns(8), columns(frames), columns(frames), columns(4),
            whole(frames + 8, 2 * N), whole(4, 2 * N), whole(frames, LANES), whole(frames, LANES),
        ],
        out_specs=[
            pair(blocks, N, LANES), pair(blocks, N, LANES), pair(N, LANES), pair(N, LANES),
            pair(8, LANES), whole(frames, LANES), whole(frames, N), whole(frames, N),
            whole(blocks, BLOCK, BLOCK), whole(blocks, LANES, BLOCK),
        ],
        out_shape=[
            shape((pairs, blocks, N, LANES), F32), shape((pairs, blocks, N, LANES), F32),
            shape((pairs, N, LANES), F32), shape((pairs, N, LANES), F32),
            shape((pairs, 8, LANES), F32), shape((frames, LANES), F32),
            shape((frames, N), F32), shape((frames, N), F32),
            shape((blocks, BLOCK, BLOCK), F32), shape((blocks, LANES, BLOCK), F32),
        ],
        scratch_shapes=[pltpu.VMEM((frames + 8, LANES), F32)]
        + [pltpu.VMEM((blocks, N, BLOCK), BF16)] * 4,
        compiler_params=pltpu.CompilerParams(vmem_limit_bytes=VMEM_LIMIT),
        name="terms",
    )(x_halo, x_raw, d_out, conv_x, bc_ext, conv_bc, s_pad, la_pad)

    in_vmem = pl.BlockSpec(memory_space=pltpu.VMEM)
    pieces = (pairs * 2, N // 2, LANES)
    state_in, grad_in = pl.pallas_call(
        lambda *refs: chain_kernel(size, *refs),
        in_specs=[in_vmem] * 3,
        out_specs=[in_vmem] * 2,
        out_shape=[shape(pieces, F32)] * 2,
        scratch_shapes=[pltpu.VMEM(pieces, F32)] * 4
        + [pltpu.SemaphoreType.DMA((pieces[0],))] * 4,
        compiler_params=pltpu.CompilerParams(
            collective_id=0, has_side_effects=True, vmem_limit_bytes=VMEM_LIMIT
        ),
        name="chain",
    )(ls.reshape(pieces), lg.reshape(pieces), dec)
    state_in = state_in.reshape(pairs, N, LANES)
    grad_in = grad_in.reshape(pairs, N, LANES)

    layer_out, grad_x, tail, first, tap_grad, skip_grad, bc_local, u, v, bnd = pl.pallas_call(
        main_kernel,
        grid=(pairs,),
        in_specs=[
            columns(8), columns(frames), columns(frames), columns(4), columns(8),
            whole(frames, LANES), whole(frames, LANES), whole(blocks, LANES, BLOCK),
            whole(frames, N), whole(frames, N), whole(blocks, BLOCK, BLOCK),
            pair(blocks, N, LANES), pair(blocks, N, LANES), pair(N, LANES), pair(N, LANES),
        ],
        out_specs=[
            columns(frames), columns(frames), columns(8), columns(8), columns(4), columns(8),
            whole(frames, 2 * N), whole(frames, LANES), whole(frames, LANES),
            whole(blocks, 8, LANES),
        ],
        out_shape=[
            shape((frames, width), BF16), shape((frames, width), BF16),
            shape((8, width), F32), shape((8, width), F32), shape((4, width), F32),
            shape((8, width), F32), shape((frames, 2 * N), F32),
            shape((frames, LANES), F32), shape((frames, LANES), F32),
            shape((blocks, 8, LANES), F32),
        ],
        scratch_shapes=[
            pltpu.VMEM((frames + 8, LANES), F32), pltpu.VMEM((frames + 8, LANES), F32),
            pltpu.VMEM((frames, LANES), F32), pltpu.VMEM((blocks, BLOCK, BLOCK), F32),
        ]
        + [pltpu.VMEM((frames, N), BF16)] * 4,
        compiler_params=pltpu.CompilerParams(vmem_limit_bytes=VMEM_LIMIT),
        name="main",
    )(
        x_halo, x_raw, d_out, conv_x, skip_wide, s_pad, run, runt,
        b_act, c_act, scores, bs, bg, state_in, grad_in,
    )

    heads = lax.axis_size("head")
    bc_total = pl.pallas_call(
        lambda *refs: head_sum_kernel(heads, *refs),
        in_specs=[in_vmem],
        out_specs=in_vmem,
        out_shape=shape((frames, 2 * N), F32),
        scratch_shapes=[pltpu.VMEM((heads, frames // heads, 2 * N), F32)]
        + [pltpu.SemaphoreType.DMA((2, heads))] * 4,
        compiler_params=pltpu.CompilerParams(
            collective_id=1, has_side_effects=True, vmem_limit_bytes=VMEM_LIMIT
        ),
        name="head_sum",
    )(bc_local)

    bc_pre = conv_bc[0] * bc_ext[5 : 5 + frames]
    for k in range(1, 4):
        bc_pre = bc_pre + conv_bc[k] * bc_ext[5 + k : 5 + k + frames]
    gate = jax.nn.sigmoid(bc_pre)
    bc_grad = bc_total * (gate * (1.0 + bc_pre * (1.0 - gate)))
    conv_bc_grad = jnp.stack(
        [jnp.sum(bc_grad * bc_ext[5 + k : 5 + k + frames], axis=0) for k in range(4)]
    )
    after = shifted(jnp.concatenate([first[:margin], bc_grad[:margin]], axis=1), "seq", -1)
    bc_spread = jnp.concatenate([bc_grad, after[:, width:]], axis=0)
    grad_bc = conv_bc[0] * bc_spread[3 : 3 + frames]
    for k in range(1, 4):
        grad_bc = grad_bc + conv_bc[k] * bc_spread[3 - k : 3 - k + frames]
    x_after = jnp.pad(after[:, :width], ((margin, 0), (0, 0)))
    patch = tail[8 - margin :]
    for k in range(margin):
        patch = patch + conv_x[k] * x_after[3 - k : 6 - k]
    grad_x = lax.dynamic_update_slice(grad_x, patch.astype(BF16), (frames - margin, 0))

    u = u[:, :head_count]
    v = v[:, :head_count]
    net = (u - step_size * v).reshape(blocks, BLOCK, head_count)
    upper = (jnp.arange(BLOCK)[:, None] <= jnp.arange(BLOCK)[None, :]).astype(F32)
    g_log = jnp.einsum("tq,kqh->kth", upper, net, precision=lax.Precision.HIGHEST)
    g_log = (g_log + bnd[:, 0:1, :head_count]).reshape(frames, head_count)
    grad_steps = (v - g_log * rates) * jax.nn.sigmoid(raw_sum)
    skip_part = jnp.sum(skip_grad[0].reshape(head_count, P_SIZE), axis=1)
    flat = jnp.concatenate(
        [
            tap_grad.reshape(-1),
            conv_bc_grad.reshape(-1),
            jnp.sum(grad_steps, axis=0),
            jnp.sum(g_log * log_decay, axis=0),
            skip_part,
        ]
    )
    lines = -(-flat.shape[0] // (8 * LANES)) * 8
    flat = jnp.pad(flat, (0, lines * LANES - flat.shape[0])).reshape(lines, LANES)
    summed = pl.pallas_call(
        lambda *refs: share_kernel(size, *refs),
        in_specs=[in_vmem],
        out_specs=in_vmem,
        out_shape=shape((lines, LANES), F32),
        scratch_shapes=[pltpu.VMEM((size, lines, LANES), F32)]
        + [pltpu.SemaphoreType.DMA((size,))] * 2,
        compiler_params=pltpu.CompilerParams(
            collective_id=2, has_side_effects=True, vmem_limit_bytes=VMEM_LIMIT
        ),
        name="share",
    )(flat).reshape(-1)
    cuts = [4 * width, 8 * N, head_count, head_count, head_count]
    parts = []
    at = 0
    for cut in cuts:
        parts.append(summed[at : at + cut])
        at += cut
    return (
        layer_out,
        grad_x,
        grad_bc,
        grad_steps,
        parts[0].reshape(4, width),
        parts[1].reshape(4, 2 * N),
        parts[2],
        parts[3],
        parts[4],
    )


def solution(mesh):
    placed = (
        P("seq", "head"),
        P("seq", None),
        P("seq", "head"),
        P(None, "head"),
        P(),
        P("head"),
        P("head"),
        P("head"),
        P("seq", "head"),
    )
    return jax.shard_map(
        local,
        mesh=mesh,
        in_specs=placed,
        out_specs=(
            P("seq", "head"),
            P("seq", "head"),
            P("seq", None),
            P("seq", "head"),
            P(None, "head"),
            P(),
            P("head"),
            P("head"),
            P("head"),
        ),
        check_vma=False,
    )
```
